32 devices in a mesh: seq: 8 (over z, y), kvh: 4 (over x, core).
Axes of the slice: x: 2, y: 2, z: 4, core: 2. Of those that a mesh axis runs over, the one named last changes fastest.
Arguments:
- queries: bfloat16 [4096, 4096], P(('seq', 'kvh')), may hold values from -5 to 5
- key_rows: bfloat16 [4096, 2048], P(('seq', 'kvh')), may hold values from -6 to 6
- value_rows: bfloat16 [4096, 2048], P(('seq', 'kvh')), may hold values from -6 to 6
- grad_out: bfloat16 [4096, 4096], P(('seq', 'kvh')), may hold values from -6 to 6
Outputs:
- attended: bfloat16 [4096, 4096], P(('seq', 'kvh'))
- grad_queries: bfloat16 [4096, 4096], P(('seq', 'kvh'))
- grad_keys: bfloat16 [4096, 2048], P(('seq', 'kvh'))
- grad_values: bfloat16 [4096, 2048], P(('seq', 'kvh'))
The draws below stay inside these ranges and needn't reach their ends.
All inputs are finite; a program needn't handle non-finite values.
Results may differ from the reference program's by a relative error of at most 0.012.
Values may be sent and summed in bfloat16 or wider, within the bound.
No kernel may reach another device: no remote copies, remote signals or barrier semaphores. Data moves between devices by JAX's collectives and lax.ppermute only.
A program may use at most 128 MiB of HBM per device.

```python
import jax
import jax.numpy as jnp
from jax import lax

QHEADS = 32
KVHEADS = 16
HEAD_DIM = 128
WINDOW = 1024
TOKENS = 4096


def draw_queries(key, part):
    base = jax.random.normal(jax.random.fold_in(key, 1), (TOKENS, KVHEADS, 2, HEAD_DIM), jnp.float32)
    base = jnp.clip(base, -5.0, 5.0)
    return base.reshape(TOKENS, QHEADS * HEAD_DIM).astype(jnp.bfloat16)


def draw_key_rows(key, part):
    base = jax.random.normal(jax.random.fold_in(key, 2), (TOKENS, KVHEADS, HEAD_DIM), jnp.float32)
    base = jnp.clip(base, -5.0, 5.0)
    return base.reshape(TOKENS, KVHEADS * HEAD_DIM).astype(jnp.bfloat16)


def level_of(rng, extent, split, smallest, top_value):
    level, own = 1.0, jax.random.fold_in(rng, 6)
    for axis_at, blocks in split:
        heights = jnp.exp(jax.random.uniform(jax.random.fold_in(own, axis_at), (blocks,), jnp.float32, smallest / len(split), top_value / len(split)))
        level = level * jnp.repeat(heights, extent[axis_at] // blocks).reshape([-1 if axis == axis_at else 1 for axis in range(len(extent))])
    return level


def gaussian(own_key, dims, scale, limit, split=(), kind=jnp.bfloat16):
    array = jax.random.normal(own_key, dims, jnp.float32) * scale
    if len(split) > 0:
        array = level_of(own_key, dims, split, -0.22, 0.18) * array
    return jnp.clip(array, min=-limit, max=limit).astype(kind)


def setup_inputs(seed: int = 0) -> dict:
    seeds = jax.random.split(jax.random.key(seed), 5)
    queries = draw_queries(jax.random.fold_in(seeds[4], 71), 0)
    key_rows = draw_key_rows(jax.random.fold_in(seeds[4], 71), 0)
    value_rows = gaussian(seeds[2], (TOKENS, KVHEADS * HEAD_DIM), 1.0, 6.0, ((0, 32),))
    grad_out = gaussian(seeds[3], (TOKENS, QHEADS * HEAD_DIM), 1.0, 6.0, ((0, 32),))
    return {"queries": queries, "key_rows": key_rows, "value_rows": value_rows, "grad_out": grad_out}


score_scale = 168.0 ** -0.5


def reference(queries, key_rows, value_rows, grad_out):
    block = WINDOW // 2
    span = WINDOW + block
    blocks = TOKENS // block
    kv_count = key_rows.shape[1] // HEAD_DIM
    width_kv = key_rows.shape[1]
    padding = jnp.zeros((WINDOW, width_kv), key_rows.dtype)
    keys_pad = jnp.concatenate([padding, key_rows], axis=0)
    values_pad = jnp.concatenate([padding, value_rows], axis=0)
    highest = lax.Precision.HIGHEST

    def one_block(totals, number):
        grad_k_acc, grad_v_acc = totals
        start_row = (number * block).astype(jnp.int32)
        q_blk = lax.dynamic_slice_in_dim(queries, start_row, block, 0).astype(jnp.float32).reshape(block, kv_count, 2, HEAD_DIM)
        o_blk = lax.dynamic_slice_in_dim(grad_out, start_row, block, 0).astype(jnp.float32).reshape(block, kv_count, 2, HEAD_DIM)
        k_blk = lax.dynamic_slice_in_dim(keys_pad, start_row, span, 0).astype(jnp.float32).reshape(span, kv_count, HEAD_DIM)
        v_blk = lax.dynamic_slice_in_dim(values_pad, start_row, span, 0).astype(jnp.float32).reshape(span, kv_count, HEAD_DIM)
        query_pos = start_row + jnp.arange(block, dtype=jnp.int32)
        key_pos = start_row - WINDOW + jnp.arange(span, dtype=jnp.int32)
        allowed = (key_pos[None, :] <= query_pos[:, None]) & (query_pos[:, None] - key_pos[None, :] < WINDOW) & (key_pos[None, :] >= 0)
        scores = jnp.einsum("rgjd,kgd->gjrk", q_blk, k_blk, precision=highest) * score_scale
        scores = jnp.where(allowed[None, None], scores, -jnp.inf)
        row_max = jnp.max(scores, axis=-1, keepdims=True)
        exponent = jnp.exp(scores - row_max)
        weights = exponent / jnp.sum(exponent, axis=-1, keepdims=True)
        weights_low = lax.optimization_barrier(weights.astype(jnp.bfloat16)).astype(jnp.float32)
        out_blk = jnp.einsum("gjrk,kgd->rgjd", weights_low, v_blk, precision=highest)
        grad_weights = jnp.einsum("rgjd,kgd->gjrk", o_blk, v_blk, precision=highest)
        row_delta = jnp.sum(weights * grad_weights, axis=-1, keepdims=True)
        grad_scores = lax.optimization_barrier((weights * (grad_weights - row_delta)).astype(jnp.bfloat16)).astype(jnp.float32)
        dq_blk = jnp.einsum("gjrk,kgd->rgjd", grad_scores, k_blk, precision=highest) * score_scale
        dk_part = jnp.einsum("gjrk,rgjd->kgd", grad_scores, q_blk, precision=highest) * score_scale
        dv_part = jnp.einsum("gjrk,rgjd->kgd", weights_low, o_blk, precision=highest)
        old_k = lax.dynamic_slice_in_dim(grad_k_acc, start_row, span, 0)
        old_v = lax.dynamic_slice_in_dim(grad_v_acc, start_row, span, 0)
        grad_k_acc = lax.dynamic_update_slice_in_dim(grad_k_acc, old_k + dk_part.reshape(span, width_kv), start_row, 0)
        grad_v_acc = lax.dynamic_update_slice_in_dim(grad_v_acc, old_v + dv_part.reshape(span, width_kv), start_row, 0)
        outputs = (out_blk.reshape(block, -1).astype(jnp.bfloat16), dq_blk.reshape(block, -1).astype(jnp.bfloat16))
        return (grad_k_acc, grad_v_acc), outputs

    initial = (jnp.zeros((TOKENS + WINDOW, width_kv), jnp.float32), jnp.zeros((TOKENS + WINDOW, width_kv), jnp.float32))
    totals, outputs = lax.scan(one_block, initial, jnp.arange(blocks, dtype=jnp.int32))
    attended = outputs[0].reshape(TOKENS, -1)
    grad_queries = outputs[1].reshape(TOKENS, -1)
    grad_keys = totals[0][WINDOW:].astype(jnp.bfloat16)
    grad_values = totals[1][WINDOW:].astype(jnp.bfloat16)
    return (attended, grad_queries, grad_keys, grad_values)
```

```python
import functools

import jax
import jax.numpy as jnp
from jax import lax
from jax.experimental import pallas as pl
from jax.experimental.pallas import tpu as pltpu
from jax.sharding import PartitionSpec as P

HEAD_DIM = 128
WINDOW = 1024
BLOCK = 128
CHUNKS = WINDOW // BLOCK + 1
SCORE_SCALE = 168.0 ** (-0.5)
EXP2_SCALE = SCORE_SCALE * 1.4426950408889634
EXCLUDED = -1e30
VMEM_BYTES = 56 * 2**20

NN = (((1,), (0,)), ((), ()))
NT = (((1,), (1,)), ((), ()))
TN = (((0,), (0,)), ((), ()))

VMEM = pl.BlockSpec(memory_space=pltpu.VMEM)
SMEM = pl.BlockSpec(memory_space=pltpu.SMEM)


def dot(left, right, dims):
    return lax.dot_general(left, right, dims, preferred_element_type=jnp.float32)


def attention_kernel(
    heads, first_ref, qo_ref, halo_ref, own_ref, ao_ref, dhalo_ref, down_ref, keys, values, acc_k, acc_v
):
    rows = own_ref.shape[0]
    width = heads * HEAD_DIM
    for h in range(heads):
        cols = slice(h * HEAD_DIM, (h + 1) * HEAD_DIM)
        vcols = slice(width + h * HEAD_DIM, width + (h + 1) * HEAD_DIM)
        keys[h, :WINDOW] = halo_ref[:, cols]
        keys[h, WINDOW:] = own_ref[:, cols]
        values[h, :WINDOW] = halo_ref[:, vcols]
        values[h, WINDOW:] = own_ref[:, vcols]
    acc_k[...] = jnp.zeros_like(acc_k)
    acc_v[...] = jnp.zeros_like(acc_v)
    key_at = lax.broadcasted_iota(jnp.int32, (BLOCK, 2 * BLOCK), 0)
    query_at = lax.broadcasted_iota(jnp.int32, (BLOCK, 2 * BLOCK), 1) & (BLOCK - 1)
    first = first_ref[0]

    def unit(h, i):
        start = pl.multiple_of(i * BLOCK, BLOCK)
        span = pl.ds(start, CHUNKS * BLOCK)
        here = pl.ds(start, BLOCK)
        qcol = 2 * h * HEAD_DIM
        ocol = 2 * width + qcol

        def both(col):
            return jnp.concatenate(
                [qo_ref[here, col : col + HEAD_DIM], qo_ref[here, col + HEAD_DIM : col + 2 * HEAD_DIM]], 0
            )

        q_rows, o_rows = both(qcol), both(ocol)
        k_rows, v_rows = keys[h, span, :], values[h, span, :]
        scores = dot(k_rows, q_rows, NT)
        parts = [scores[c * BLOCK : (c + 1) * BLOCK] for c in range(CHUNKS)]
        parts[0] = jnp.where(key_at > query_at, parts[0], EXCLUDED)
        parts[-1] = jnp.where(key_at <= query_at, parts[-1], EXCLUDED)
        bias = [
            jnp.where((first > 0) & (i + c < WINDOW // BLOCK), EXCLUDED, 0.0).astype(jnp.float32)
            for c in range(CHUNKS - 1)
        ]
        top = jnp.max(parts[-1], axis=0, keepdims=True)
        for c in range(CHUNKS - 1):
            top = jnp.maximum(top, jnp.max(parts[c], axis=0, keepdims=True) + bias[c])
        top = top * EXP2_SCALE
        total = jnp.zeros_like(top)
        exps = []
        for c in range(CHUNKS):
            shift = top if c == CHUNKS - 1 else top - bias[c]
            exps.append(jnp.exp2(parts[c] * EXP2_SCALE - shift))
            total = total + jnp.sum(exps[c], axis=0, keepdims=True)
        inverse = 1.0 / total
        weights = [e * inverse for e in exps]
        weights_low = jnp.concatenate([w.astype(jnp.bfloat16) for w in weights], 0)
        grad_weights = dot(v_rows, o_rows, NT)
        delta = jnp.zeros_like(total)
        for c in range(CHUNKS):
            delta = delta + jnp.sum(weights[c] * grad_weights[c * BLOCK : (c + 1) * BLOCK], axis=0, keepdims=True)
        grad_scores = jnp.concatenate(
            [
                (weights[c] * (grad_weights[c * BLOCK : (c + 1) * BLOCK] - delta)).astype(jnp.bfloat16)
                for c in range(CHUNKS)
            ],
            0,
        )
        attended = dot(weights_low, v_rows, TN).astype(jnp.bfloat16)
        grad_q = (dot(grad_scores, k_rows, TN) * SCORE_SCALE).astype(jnp.bfloat16)
        for j in range(2):
            part = slice(j * BLOCK, (j + 1) * BLOCK)
            ao_ref[here, qcol + j * HEAD_DIM : qcol + (j + 1) * HEAD_DIM] = attended[part]
            ao_ref[here, ocol + j * HEAD_DIM : ocol + (j + 1) * HEAD_DIM] = grad_q[part]
        acc_v[h, span, :] += dot(weights_low, o_rows, NN)
        acc_k[h, span, :] += dot(grad_scores, q_rows, NN)

    def step(i, carry):
        for h in range(heads):
            unit(h, i)
        return carry

    lax.fori_loop(0, rows // BLOCK, step, 0)
    for h in range(heads):
        cols = slice(h * HEAD_DIM, (h + 1) * HEAD_DIM)
        vcols = slice(width + h * HEAD_DIM, width + (h + 1) * HEAD_DIM)
        dhalo_ref[:, cols] = (acc_k[h, :WINDOW] * SCORE_SCALE).astype(jnp.bfloat16)
        dhalo_ref[:, vcols] = acc_v[h, :WINDOW].astype(jnp.bfloat16)
        down_ref[:, cols] = acc_k[h, WINDOW:] * SCORE_SCALE
        down_ref[:, vcols] = acc_v[h, WINDOW:]


def attention(first, qo, halo, own):
    rows = own.shape[0]
    heads = own.shape[1] // (2 * HEAD_DIM)
    window = (heads, WINDOW + rows, HEAD_DIM)
    return pl.pallas_call(
        functools.partial(attention_kernel, heads),
        out_shape=(
            jax.ShapeDtypeStruct(qo.shape, jnp.bfloat16),
            jax.ShapeDtypeStruct(halo.shape, jnp.bfloat16),
            jax.ShapeDtypeStruct(own.shape, jnp.float32),
        ),
        in_specs=[SMEM, VMEM, VMEM, VMEM],
        out_specs=(VMEM, VMEM, VMEM),
        scratch_shapes=[
            pltpu.VMEM(window, jnp.bfloat16),
            pltpu.VMEM(window, jnp.bfloat16),
            pltpu.VMEM(window, jnp.float32),
            pltpu.VMEM(window, jnp.float32),
        ],
        compiler_params=pltpu.CompilerParams(vmem_limit_bytes=VMEM_BYTES),
        name="attention",
    )(first, qo, halo, own)


def pack_kernel(a_ref, b_ref, out_ref):
    groups, _, width = out_ref.shape
    half = width // 2
    for g in range(groups):
        out_ref[g, :, :half] = a_ref[:, g * half : (g + 1) * half]
        out_ref[g, :, half:] = b_ref[:, g * half : (g + 1) * half]


def pack(a, b, groups):
    rows, cols = a.shape
    return pl.pallas_call(
        pack_kernel,
        out_shape=jax.ShapeDtypeStruct((groups, rows, 2 * cols // groups), a.dtype),
        in_specs=[VMEM, VMEM],
        out_specs=VMEM,
        compiler_params=pltpu.CompilerParams(vmem_limit_bytes=VMEM_BYTES),
        name="pack",
    )(a, b)


def unpack_kernel(x_ref, a_ref, b_ref):
    groups, _, width = x_ref.shape
    half = width // 2
    for g in range(groups):
        a_ref[:, g * half : (g + 1) * half] = x_ref[g, :, :half]
        b_ref[:, g * half : (g + 1) * half] = x_ref[g, :, half:]


def unpack(x):
    groups, rows, width = x.shape
    shape = jax.ShapeDtypeStruct((rows, groups * width // 2), x.dtype)
    return pl.pallas_call(
        unpack_kernel,
        out_shape=(shape, shape),
        in_specs=[VMEM],
        out_specs=(VMEM, VMEM),
        compiler_params=pltpu.CompilerParams(vmem_limit_bytes=VMEM_BYTES),
        name="unpack",
    )(x)


def body(queries, key_rows, value_rows, grad_out):
    shards, split = lax.axis_size("seq"), lax.axis_size("kvh")
    rows = queries.shape[0]
    span = WINDOW // (rows * split)
    members = span * split
    groups = [[g * members + i for i in range(members)] for g in range(shards // span)]
    first = (lax.axis_index("seq") < span).astype(jnp.int32).reshape(1)

    def exchange(x):
        return lax.all_to_all(x, ("seq", "kvh"), 0, 0, tiled=True, axis_index_groups=groups)

    own = exchange(pack(key_rows, value_rows, members)).reshape(WINDOW, -1)
    halo = lax.ppermute(own, "seq", [(i, i + span) for i in range(shards - span)])
    qo = exchange(pack(queries, grad_out, members)).reshape(WINDOW, -1)
    outs, dhalo, down = attention(first, qo, halo, own)
    back = lax.ppermute(dhalo, "seq", [(i + span, i) for i in range(shards - span)])
    attended, grad_q = unpack(exchange(outs.reshape(members, rows, -1)))
    total = (down + back.astype(jnp.float32)).astype(jnp.bfloat16)
    grad_k, grad_v = unpack(exchange(total.reshape(members, rows, -1)))
    return (attended, grad_q, grad_k, grad_v)


def solution(mesh):
    placed = P(("seq", "kvh"), None)
    return jax.shard_map(
        body, mesh=mesh, in_specs=(placed,) * 4, out_specs=(placed,) * 4, check_vma=False
    )
```

```python
import functools

import jax
import jax.numpy as jnp
from jax import lax
from jax.experimental import pallas as pl
from jax.experimental.pallas import tpu as pltpu
from jax.sharding import PartitionSpec as P

HEAD_DIM = 128
PAIR = 2 * HEAD_DIM
WINDOW = 1024
BLOCK = 128
CHUNKS = WINDOW // BLOCK + 1
SCORE_SCALE = 168.0 ** (-0.5)
EXP2_SCALE = SCORE_SCALE * 1.4426950408889634
EXCLUDED = -1e30
ONES = 16

NN = (((1,), (0,)), ((), ()))
NT = (((1,), (1,)), ((), ()))

VMEM = pl.BlockSpec(memory_space=pltpu.VMEM)
SMEM = pl.BlockSpec(memory_space=pltpu.SMEM)
ANY = pl.BlockSpec(memory_space=pl.ANY)
HBM = pl.BlockSpec(memory_space=pltpu.HBM)


def dot(left, right, dims):
    return lax.dot_general(left, right, dims, preferred_element_type=jnp.float32)


def side_by_side(x):
    return jnp.concatenate([x[:, :HEAD_DIM].T, x[:, HEAD_DIM:].T], 1)


def attention_kernel(
    head, first_ref, qo_hbm, halo_hbm, own_hbm, ao_hbm, dhalo_hbm, down_hbm,
    kv, qo, ao, dhalo, keys_t, values_t, acc_k, acc_v, exps0, exps1, q_turned, o_turned, in_sem, q_sem, out_sem,
):
    rows = qo.shape[0]
    blocks = rows // BLOCK
    whole = WINDOW // BLOCK
    exps = (exps0, exps1)

    def at(i):
        return pl.ds(pl.multiple_of(i * BLOCK, BLOCK), BLOCK)

    def span(i):
        return pl.ds(pl.multiple_of(i * BLOCK, BLOCK), CHUNKS * BLOCK)

    def qo_copy(i):
        return pltpu.make_async_copy(qo_hbm.at[at(i)], qo.at[at(i)], q_sem.at[i])

    def ao_copy(i):
        return pltpu.make_async_copy(ao.at[at(i)], ao_hbm.at[at(i)], out_sem.at[0, i])

    def dhalo_copy(i):
        return pltpu.make_async_copy(dhalo.at[at(i)], dhalo_hbm.at[at(i)], out_sem.at[1, i])

    halo_copy = pltpu.make_async_copy(halo_hbm, kv.at[pl.ds(0, WINDOW)], in_sem.at[0])
    own_copy = pltpu.make_async_copy(
        own_hbm.at[:, pl.ds(head * PAIR, PAIR)], kv.at[pl.ds(WINDOW, rows)], in_sem.at[1]
    )
    halo_copy.start()
    own_copy.start()
    for i in range(blocks):
        qo_copy(i).start()

    ones_row = lax.broadcasted_iota(jnp.int32, (ONES, values_t.shape[1]), 0) == 0
    values_t[HEAD_DIM:, :] = jnp.where(ones_row, 1.0, 0.0).astype(jnp.bfloat16)
    acc_k[:, : WINDOW + BLOCK] = jnp.zeros((HEAD_DIM, WINDOW + BLOCK), jnp.float32)
    acc_v[:, : WINDOW + BLOCK] = jnp.zeros((HEAD_DIM, WINDOW + BLOCK), jnp.float32)
    exps1[...] = jnp.ones_like(exps1)
    q_turned[...] = jnp.zeros_like(q_turned)
    o_turned[...] = jnp.zeros_like(o_turned)
    key_at = lax.broadcasted_iota(jnp.int32, (BLOCK, 2 * BLOCK), 0)
    query_at = lax.broadcasted_iota(jnp.int32, (BLOCK, 2 * BLOCK), 1) & (BLOCK - 1)
    first = first_ref[0]

    def turn(target, source):
        keys_t[:, at(target)] = kv[at(source), :HEAD_DIM].T
        values_t[:HEAD_DIM, at(target)] = kv[at(source), HEAD_DIM:].T

    halo_copy.wait()
    own_copy.wait()
    for c in range(whole + 1):
        turn(c, c)

    def scores_of(slot, i):
        q_t, o_t = side_by_side(qo[at(i), :PAIR]), side_by_side(qo[at(i), PAIR:])
        q_turned[slot] = q_t
        o_turned[slot] = o_t
        bias = [
            jnp.where((first > 0) & (i + c < whole), EXCLUDED, 0.0).astype(jnp.float32) for c in range(CHUNKS - 1)
        ]
        scores = dot(kv[span(i), :HEAD_DIM], q_t, NN)
        parts = [scores[c * BLOCK : (c + 1) * BLOCK] for c in range(CHUNKS)]
        parts[0] = jnp.where(key_at > query_at, parts[0], EXCLUDED)
        parts[-1] = jnp.where(key_at <= query_at, parts[-1], EXCLUDED)
        top = jnp.max(parts[-1], axis=0, keepdims=True)
        for c in range(CHUNKS - 1):
            top = jnp.maximum(top, jnp.max(parts[c], axis=0, keepdims=True) + bias[c])
        top = top * EXP2_SCALE
        return parts, [top - b for b in bias] + [top]

    def exponentials(slot, parts, shifts):
        for c in range(CHUNKS):
            exps[slot][c * BLOCK : (c + 1) * BLOCK] = jnp.exp2(parts[c] * EXP2_SCALE - shifts[c]).astype(jnp.bfloat16)

    def attended_of(slot, i):
        out = dot(values_t[:, span(i)], exps[slot][...], NN)
        inverse = 1.0 / out[HEAD_DIM : HEAD_DIM + 1]
        out = out[:HEAD_DIM] * inverse
        grad_out = o_turned[slot].astype(jnp.float32)
        delta = jnp.sum(out * grad_out, axis=0, keepdims=True)
        out = out.astype(jnp.bfloat16)
        ao[at(i), :HEAD_DIM] = out[:, :BLOCK].T
        ao[at(i), HEAD_DIM:PAIR] = out[:, BLOCK:].T
        o_scaled = (grad_out * inverse).astype(jnp.bfloat16)
        q_scaled = (q_turned[slot].astype(jnp.float32) * inverse).astype(jnp.bfloat16)
        return inverse, delta, o_scaled, q_scaled

    def gradients(slot, i, inverse, delta, o_scaled, q_scaled):
        grad_weights = dot(kv[span(i), HEAD_DIM:], o_turned[slot], NN)
        grad_scores = []
        for c in range(CHUNKS):
            part = slice(c * BLOCK, (c + 1) * BLOCK)
            grad_scores.append(
                (exps[slot][part].astype(jnp.float32) * (grad_weights[part] - delta)).astype(jnp.bfloat16)
            )
        grad_scores = jnp.concatenate(grad_scores, 0)
        acc_v[:, span(i)] += dot(o_scaled, exps[slot][...], NT)
        grad_q = (dot(keys_t[:, span(i)], grad_scores, NN) * (inverse * SCORE_SCALE)).astype(jnp.bfloat16)
        ao[at(i), PAIR : PAIR + HEAD_DIM] = grad_q[:, :BLOCK].T
        ao[at(i), PAIR + HEAD_DIM :] = grad_q[:, BLOCK:].T
        acc_k[:, span(i)] += dot(q_scaled, grad_scores, NT)

    def flush(i):
        dhalo[at(i), :HEAD_DIM] = (acc_k[:, at(i)] * SCORE_SCALE).astype(jnp.bfloat16).T
        dhalo[at(i), HEAD_DIM:] = acc_v[:, at(i)].astype(jnp.bfloat16).T

    def both(slot, i, before):
        known = attended_of(1 - slot, before)
        parts, shifts = scores_of(slot, i)
        exponentials(slot, parts, shifts)
        gradients(1 - slot, before, *known)
        flush(before)
        turn(i + whole + 1, jnp.minimum(i + whole + 1, whole + blocks - 1))
        acc_k[:, at(i + whole + 1)] = jnp.zeros((HEAD_DIM, BLOCK), jnp.float32)
        acc_v[:, at(i + whole + 1)] = jnp.zeros((HEAD_DIM, BLOCK), jnp.float32)

    def step(j, carry):
        i = 2 * j
        qo_copy(i).wait()
        qo_copy(i + 1).wait()
        both(0, i, jnp.maximum(i - 1, 0))
        both(1, i + 1, i)

        @pl.when(j > 0)
        def _():
            ao_copy(i - 1).start()
            dhalo_copy(i - 1).start()

        ao_copy(i).start()
        dhalo_copy(i).start()
        return carry

    lax.fori_loop(0, blocks // 2, step, 0)
    gradients(1, blocks - 1, *attended_of(1, blocks - 1))
    flush(blocks - 1)
    ao_copy(blocks - 1).start()
    dhalo_copy(blocks - 1).start()
    own_k = pltpu.make_async_copy(acc_k.at[:, pl.ds(WINDOW, rows)], down_hbm.at[0], in_sem.at[0])
    own_v = pltpu.make_async_copy(acc_v.at[:, pl.ds(WINDOW, rows)], down_hbm.at[1], in_sem.at[1])
    own_k.start()
    own_v.start()
    for i in range(blocks):
        ao_copy(i).wait()
        dhalo_copy(i).wait()
    own_k.wait()
    own_v.wait()


def attention(head, first, qo, halo, own):
    rows = own.shape[0]
    blocks = rows // BLOCK
    reach = WINDOW + rows
    bf16, f32 = jnp.bfloat16, jnp.float32
    return pl.pallas_call(
        functools.partial(attention_kernel, head),
        out_shape=(
            jax.ShapeDtypeStruct(qo.shape, bf16),
            jax.ShapeDtypeStruct(halo.shape, bf16),
            jax.ShapeDtypeStruct((2, HEAD_DIM, rows), f32),
        ),
        in_specs=[SMEM, ANY, ANY, ANY],
        out_specs=(HBM, HBM, HBM),
        scratch_shapes=[
            pltpu.VMEM((reach, PAIR), bf16),
            pltpu.VMEM(qo.shape, bf16),
            pltpu.VMEM(qo.shape, bf16),
            pltpu.VMEM(halo.shape, bf16),
            pltpu.VMEM((HEAD_DIM, reach + BLOCK), bf16),
            pltpu.VMEM((HEAD_DIM + ONES, reach + BLOCK), bf16),
            pltpu.VMEM((HEAD_DIM, reach + BLOCK), f32),
            pltpu.VMEM((HEAD_DIM, reach + BLOCK), f32),
            pltpu.VMEM((CHUNKS * BLOCK, 2 * BLOCK), bf16),
            pltpu.VMEM((CHUNKS * BLOCK, 2 * BLOCK), bf16),
            pltpu.VMEM((2, HEAD_DIM, 2 * BLOCK), bf16),
            pltpu.VMEM((2, HEAD_DIM, 2 * BLOCK), bf16),
            pltpu.SemaphoreType.DMA((2,)),
            pltpu.SemaphoreType.DMA((blocks,)),
            pltpu.SemaphoreType.DMA((2, blocks)),
        ],
        compiler_params=pltpu.CompilerParams(vmem_limit_bytes=32 * 2**20),
        cost_estimate=pl.CostEstimate(flops=10**10, bytes_accessed=4 * 2**20, transcendentals=0),
        name="attention",
    )(first, qo, halo, own)


def interleave_kernel(width, parts, *refs):
    *arrays, out = refs
    for g in range(out.shape[0]):
        for n, (which, start, stride) in enumerate(parts):
            first = g * stride + start
            out[g, :, n * width : (n + 1) * width] = arrays[which][:, first : first + width]


def interleave(arrays, groups, width, parts):
    rows = arrays[0].shape[0]
    return pl.pallas_call(
        functools.partial(interleave_kernel, width, parts),
        out_shape=jax.ShapeDtypeStruct((groups, rows, width * len(parts)), arrays[0].dtype),
        in_specs=[VMEM] * len(arrays),
        out_specs=VMEM,
        compiler_params=pltpu.CompilerParams(vmem_limit_bytes=16 * 2**20),
        name="interleave",
    )(*arrays)


def spread_kernel(x_ref, y_ref, a_ref, b_ref):
    groups, _, width = x_ref.shape
    half = width // 2
    for g in range(groups):
        for n, ref in enumerate((x_ref, y_ref)):
            cols = slice(g * width + n * half, g * width + (n + 1) * half)
            a_ref[:, cols] = ref[g, :, :half]
            b_ref[:, cols] = ref[g, :, half:]


def spread(x, y):
    groups, rows, width = x.shape
    shape = jax.ShapeDtypeStruct((rows, groups * width), x.dtype)
    return pl.pallas_call(
        spread_kernel,
        out_shape=(shape, shape),
        in_specs=[VMEM, VMEM],
        out_specs=(VMEM, VMEM),
        compiler_params=pltpu.CompilerParams(vmem_limit_bytes=16 * 2**20),
        name="spread",
    )(x, y)


def add_kernel(own0_ref, own1_ref, back0_ref, back1_ref, out_ref):
    for h, (own, back) in enumerate(((own0_ref, back0_ref), (own1_ref, back1_ref))):
        for i in range(out_ref.shape[0] // BLOCK):
            rows = slice(i * BLOCK, (i + 1) * BLOCK)
            for n, scale in enumerate((SCORE_SCALE, 1.0)):
                total = (own[n, :, rows] * scale).T + back[rows, n * HEAD_DIM : (n + 1) * HEAD_DIM].astype(jnp.float32)
                cols = slice((2 * n + h) * HEAD_DIM, (2 * n + h + 1) * HEAD_DIM)
                out_ref[rows, cols] = total.astype(jnp.bfloat16)


def add(own, back):
    rows, width = back[0].shape
    return pl.pallas_call(
        add_kernel,
        out_shape=jax.ShapeDtypeStruct((rows, 2 * width), jnp.bfloat16),
        in_specs=[VMEM] * 4,
        out_specs=VMEM,
        compiler_params=pltpu.CompilerParams(vmem_limit_bytes=16 * 2**20),
        name="add",
    )(*own, *back)


def unpack_kernel(x_ref, a_ref, b_ref):
    groups, _, width = x_ref.shape
    half = width // 2
    for g in range(groups):
        a_ref[:, g * half : (g + 1) * half] = x_ref[g, :, :half]
        b_ref[:, g * half : (g + 1) * half] = x_ref[g, :, half:]


def unpack(x):
    groups, rows, width = x.shape
    shape = jax.ShapeDtypeStruct((rows, groups * width // 2), x.dtype)
    return pl.pallas_call(
        unpack_kernel,
        out_shape=(shape, shape),
        in_specs=[VMEM],
        out_specs=(VMEM, VMEM),
        compiler_params=pltpu.CompilerParams(vmem_limit_bytes=16 * 2**20),
        name="unpack",
    )(x)


def body(queries, key_rows, value_rows, grad_out):
    shards, split = lax.axis_size("seq"), lax.axis_size("kvh")
    rows = queries.shape[0]
    apart = WINDOW // (rows * split)
    members = apart * split
    heads = key_rows.shape[1] // (members * HEAD_DIM)
    groups = [[g * members + i for i in range(members)] for g in range(shards // apart)]
    first = (lax.axis_index("seq") < apart).astype(jnp.int32).reshape(1)

    def exchange(x):
        return lax.all_to_all(x, ("seq", "kvh"), 0, 0, tiled=True, axis_index_groups=groups)

    def onward(x):
        return lax.ppermute(x, "seq", [(i, i + apart) for i in range(shards - apart)])

    def backward(x):
        return lax.ppermute(x, "seq", [(i + apart, i) for i in range(shards - apart)])

    stride = heads * HEAD_DIM
    kv_parts = [(n, h * HEAD_DIM, stride) for h in range(heads) for n in range(2)]
    own = exchange(interleave((key_rows, value_rows), members, HEAD_DIM, kv_parts)).reshape(WINDOW, -1)
    halos = [onward(own[:, h * PAIR : (h + 1) * PAIR]) for h in range(heads)]
    outs, down, back = [], [], []
    for h in range(heads):
        qo_parts = [(n, h * PAIR, 2 * stride) for n in range(2)]
        qo = exchange(interleave((queries, grad_out), members, PAIR, qo_parts)).reshape(WINDOW, -1)
        ao, dhalo, mine = attention(h, first, qo, halos[h], own)
        if h > 0:
            ao, back[h - 1] = lax.optimization_barrier((ao, back[h - 1]))
        back.append(backward(dhalo))
        outs.append(exchange(ao.reshape(members, rows, -1)))
        down.append(mine)
    *outs, total = lax.optimization_barrier((*outs, add(down, back)))
    grad_k, grad_v = unpack(exchange(total.reshape(members, rows, -1)))
    attended, grad_q = spread(*outs)
    return (attended, grad_q, grad_k, grad_v)


def solution(mesh):
    placed = P(("seq", "kvh"), None)
    return jax.shard_map(
        body, mesh=mesh, in_specs=(placed,) * 4, out_specs=(placed,) * 4, check_vma=False
    )
```

```python
import functools

import jax
import jax.numpy as jnp
from jax import lax
from jax.experimental import pallas as pl
from jax.experimental.pallas import tpu as pltpu
from jax.sharding import PartitionSpec as P

HEAD_DIM = 128
PAIR = 2 * HEAD_DIM
WINDOW = 1024
BLOCK = 128
CHUNKS = WINDOW // BLOCK + 1
SCORE_SCALE = 168.0 ** (-0.5)
EXP2_SCALE = SCORE_SCALE * 1.4426950408889634
EXCLUDED = -1e30
ONES = 16
IN_FLIGHT = 4

NN = (((1,), (0,)), ((), ()))
NT = (((1,), (1,)), ((), ()))

VMEM = pl.BlockSpec(memory_space=pltpu.VMEM)
SMEM = pl.BlockSpec(memory_space=pltpu.SMEM)
ANY = pl.BlockSpec(memory_space=pl.ANY)
HBM = pl.BlockSpec(memory_space=pltpu.HBM)


def dot(left, right, dims):
    return lax.dot_general(left, right, dims, preferred_element_type=jnp.float32)


def side_by_side(x):
    return jnp.concatenate([x[:, :HEAD_DIM].T, x[:, HEAD_DIM:].T], 1)


def attention_kernel(
    head, pieces, place_ref, qo_hbm, halo_hbm, own_hbm, *refs
):
    ao_hbm, (dhalo_hbm, down_hbm, *refs) = refs[:pieces], refs[pieces:]
    (kv, qo, ao, dhalo, keys_t, values_t, acc_k, acc_v, exps0, exps1, q_turned, o_turned, in_sem, q_sem, out_sem) = refs
    rows = qo.shape[0]
    blocks = rows // BLOCK
    whole = WINDOW // BLOCK
    exps = (exps0, exps1)

    def at(i):
        return pl.ds(pl.multiple_of(i * BLOCK, BLOCK), BLOCK)

    def span(i):
        return pl.ds(pl.multiple_of(i * BLOCK, BLOCK), CHUNKS * BLOCK)

    def qo_copy(i):
        return pltpu.make_async_copy(qo_hbm.at[at(i)], qo.at[at(i)], q_sem.at[i])

    def ao_copy(i):
        return pltpu.make_async_copy(ao.at[at(i)], ao_hbm[0].at[at(i)], out_sem.at[0, i])

    def piece_copy(j):
        return pltpu.make_async_copy(ao.at[at(place_ref[1] ^ j)], ao_hbm[j], out_sem.at[0, j])

    def dhalo_copy(i):
        return pltpu.make_async_copy(dhalo.at[at(i)], dhalo_hbm.at[at(i)], out_sem.at[1, i])

    halo_copy = pltpu.make_async_copy(halo_hbm, kv.at[pl.ds(0, WINDOW)], in_sem.at[0])
    own_copy = pltpu.make_async_copy(
        own_hbm.at[:, pl.ds(head * PAIR, PAIR)], kv.at[pl.ds(WINDOW, rows)], in_sem.at[1]
    )
    halo_copy.start()
    own_copy.start()
    for i in range(blocks):
        qo_copy(i).start()

    ones_row = lax.broadcasted_iota(jnp.int32, (ONES, values_t.shape[1]), 0) == 0
    values_t[HEAD_DIM:, :] = jnp.where(ones_row, 1.0, 0.0).astype(jnp.bfloat16)
    acc_k[:, : WINDOW + BLOCK] = jnp.zeros((HEAD_DIM, WINDOW + BLOCK), jnp.float32)
    acc_v[:, : WINDOW + BLOCK] = jnp.zeros((HEAD_DIM, WINDOW + BLOCK), jnp.float32)
    exps1[...] = jnp.ones_like(exps1)
    q_turned[...] = jnp.zeros_like(q_turned)
    o_turned[...] = jnp.zeros_like(o_turned)
    key_at = lax.broadcasted_iota(jnp.int32, (BLOCK, 2 * BLOCK), 0)
    query_at = lax.broadcasted_iota(jnp.int32, (BLOCK, 2 * BLOCK), 1) & (BLOCK - 1)
    first = place_ref[0]

    def turn(target, source):
        keys_t[:, at(target)] = kv[at(source), :HEAD_DIM].T
        values_t[:HEAD_DIM, at(target)] = kv[at(source), HEAD_DIM:].T

    halo_copy.wait()
    own_copy.wait()
    for c in range(whole + 1):
        turn(c, c)

    def scores_of(slot, i):
        q_t, o_t = side_by_side(qo[at(i), :PAIR]), side_by_side(qo[at(i), PAIR:])
        q_turned[slot] = q_t
        o_turned[slot] = o_t
        bias = [
            jnp.where((first > 0) & (i + c < whole), EXCLUDED, 0.0).astype(jnp.float32) for c in range(CHUNKS - 1)
        ]
        scores = dot(kv[span(i), :HEAD_DIM], q_t, NN)
        parts = [scores[c * BLOCK : (c + 1) * BLOCK] for c in range(CHUNKS)]
        parts[0] = jnp.where(key_at > query_at, parts[0], EXCLUDED)
        parts[-1] = jnp.where(key_at <= query_at, parts[-1], EXCLUDED)
        top = jnp.max(parts[-1], axis=0, keepdims=True)
        for c in range(CHUNKS - 1):
            top = jnp.maximum(top, jnp.max(parts[c], axis=0, keepdims=True) + bias[c])
        top = top * EXP2_SCALE
        return parts, [top - b for b in bias] + [top]

    def exponentials(slot, parts, shifts):
        for c in range(CHUNKS):
            exps[slot][c * BLOCK : (c + 1) * BLOCK] = jnp.exp2(parts[c] * EXP2_SCALE - shifts[c]).astype(jnp.bfloat16)

    def attended_of(slot, i):
        out = dot(values_t[:, span(i)], exps[slot][...], NN)
        inverse = 1.0 / out[HEAD_DIM : HEAD_DIM + 1]
        out = out[:HEAD_DIM] * inverse
        grad_out = o_turned[slot].astype(jnp.float32)
        delta = jnp.sum(out * grad_out, axis=0, keepdims=True)
        out = out.astype(jnp.bfloat16)
        ao[at(i), :HEAD_DIM] = out[:, :BLOCK].T
        ao[at(i), HEAD_DIM:PAIR] = out[:, BLOCK:].T
        o_scaled = (grad_out * inverse).astype(jnp.bfloat16)
        q_scaled = (q_turned[slot].astype(jnp.float32) * inverse).astype(jnp.bfloat16)
        return inverse, delta, o_scaled, q_scaled

    def gradients(slot, i, inverse, delta, o_scaled, q_scaled):
        grad_weights = dot(kv[span(i), HEAD_DIM:], o_turned[slot], NN)
        grad_scores = []
        for c in range(CHUNKS):
            part = slice(c * BLOCK, (c + 1) * BLOCK)
            grad_scores.append(
                (exps[slot][part].astype(jnp.float32) * (grad_weights[part] - delta)).astype(jnp.bfloat16)
            )
        grad_scores = jnp.concatenate(grad_scores, 0)
        acc_v[:, span(i)] += dot(o_scaled, exps[slot][...], NT)
        grad_q = (dot(keys_t[:, span(i)], grad_scores, NN) * (inverse * SCORE_SCALE)).astype(jnp.bfloat16)
        ao[at(i), PAIR : PAIR + HEAD_DIM] = grad_q[:, :BLOCK].T
        ao[at(i), PAIR + HEAD_DIM :] = grad_q[:, BLOCK:].T
        acc_k[:, span(i)] += dot(q_scaled, grad_scores, NT)

    def flush(i):
        dhalo[at(i), :HEAD_DIM] = (acc_k[:, at(i)] * SCORE_SCALE).astype(jnp.bfloat16).T
        dhalo[at(i), HEAD_DIM:] = acc_v[:, at(i)].astype(jnp.bfloat16).T

    def both(slot, i, before):
        known = attended_of(1 - slot, before)
        parts, shifts = scores_of(slot, i)
        exponentials(slot, parts, shifts)
        gradients(1 - slot, before, *known)
        flush(before)
        turn(i + whole + 1, jnp.minimum(i + whole + 1, whole + blocks - 1))
        acc_k[:, at(i + whole + 1)] = jnp.zeros((HEAD_DIM, BLOCK), jnp.float32)
        acc_v[:, at(i + whole + 1)] = jnp.zeros((HEAD_DIM, BLOCK), jnp.float32)

    def step(j, carry):
        i = 2 * j
        qo_copy(i).wait()
        qo_copy(i + 1).wait()
        both(0, i, jnp.maximum(i - 1, 0))
        both(1, i + 1, i)

        @pl.when(j > 0)
        def _():
            if pieces == 1:
                ao_copy(i - 1).start()
            dhalo_copy(i - 1).start()

        if pieces == 1:
            ao_copy(i).start()
        dhalo_copy(i).start()
        return carry

    lax.fori_loop(0, blocks // 2, step, 0)
    gradients(1, blocks - 1, *attended_of(1, blocks - 1))
    flush(blocks - 1)
    dhalo_copy(blocks - 1).start()
    if pieces == 1:
        ao_copy(blocks - 1).start()
    else:
        for j in range(pieces):
            piece_copy(j).start()
    own_k = pltpu.make_async_copy(acc_k.at[:, pl.ds(WINDOW, rows)], down_hbm.at[0], in_sem.at[0])
    own_v = pltpu.make_async_copy(acc_v.at[:, pl.ds(WINDOW, rows)], down_hbm.at[1], in_sem.at[1])
    own_k.start()
    own_v.start()
    for i in range(blocks):
        (ao_copy(i) if pieces == 1 else piece_copy(i)).wait()
        dhalo_copy(i).wait()
    own_k.wait()
    own_v.wait()


def attention(head, place, qo, halo, own, pieces):
    rows = own.shape[0]
    blocks = rows // BLOCK
    reach = WINDOW + rows
    bf16, f32 = jnp.bfloat16, jnp.float32
    return pl.pallas_call(
        functools.partial(attention_kernel, head, pieces),
        out_shape=(
            *[jax.ShapeDtypeStruct((rows // pieces, qo.shape[1]), bf16)] * pieces,
            jax.ShapeDtypeStruct(halo.shape, bf16),
            jax.ShapeDtypeStruct((2, HEAD_DIM, rows), f32),
        ),
        in_specs=[SMEM, ANY, ANY, ANY],
        out_specs=(HBM,) * (pieces + 2),
        scratch_shapes=[
            pltpu.VMEM((reach, PAIR), bf16),
            pltpu.VMEM(qo.shape, bf16),
            pltpu.VMEM(qo.shape, bf16),
            pltpu.VMEM(halo.shape, bf16),
            pltpu.VMEM((HEAD_DIM, reach + BLOCK), bf16),
            pltpu.VMEM((HEAD_DIM + ONES, reach + BLOCK), bf16),
            pltpu.VMEM((HEAD_DIM, reach + BLOCK), f32),
            pltpu.VMEM((HEAD_DIM, reach + BLOCK), f32),
            pltpu.VMEM((CHUNKS * BLOCK, 2 * BLOCK), bf16),
            pltpu.VMEM((CHUNKS * BLOCK, 2 * BLOCK), bf16),
            pltpu.VMEM((2, HEAD_DIM, 2 * BLOCK), bf16),
            pltpu.VMEM((2, HEAD_DIM, 2 * BLOCK), bf16),
            pltpu.SemaphoreType.DMA((2,)),
            pltpu.SemaphoreType.DMA((blocks,)),
            pltpu.SemaphoreType.DMA((2, blocks)),
        ],
        compiler_params=pltpu.CompilerParams(vmem_limit_bytes=58 * 2**20),
        cost_estimate=pl.CostEstimate(flops=10**10, bytes_accessed=4 * 2**20, transcendentals=0),
        name="attention",
    )(place, qo, halo, own)


def interleave_kernel(width, parts, split, place_ref, *refs):
    arrays, refs = refs[:2], refs[2:]
    groups = arrays[0].shape[1] // parts[0][2]
    outs, (first, second, staged, in_sem, out_sem) = refs[: groups if split else 1], refs[groups if split else 1 :]
    half = arrays[0].shape[1] // 2
    fetched = (first, second)
    loads = []
    for n in range(2):
        for h in range(2):
            cols = pl.ds(h * half, half)
            loads.append(pltpu.make_async_copy(arrays[n].at[:, cols], fetched[n].at[:, cols], in_sem.at[2 * n + h]))
    for load in loads:
        load.start()
    if split:
        for load in loads:
            load.wait()
    stores = []
    for g in range(groups):
        if not split and g % (groups // 2) == 0:
            loads[g // (groups // 2)].wait()
            loads[2 + g // (groups // 2)].wait()
        source = place_ref[1] ^ g if split else g
        for n, (which, start, stride) in enumerate(parts):
            at = source * stride + start
            if split:
                at = pl.multiple_of(at, HEAD_DIM)
            staged[g, :, n * width : (n + 1) * width] = fetched[which][:, pl.ds(at, width)]
        stores.append(pltpu.make_async_copy(staged.at[g], outs[g] if split else outs[0].at[g], out_sem.at[g]))
        stores[g].start()
    for store in stores:
        store.wait()


def interleave(place, arrays, groups, width, parts, split=False):
    rows, cols = arrays[0].shape
    dtype = arrays[0].dtype
    out = (rows, width * len(parts))
    whole = (groups, *out)
    return pl.pallas_call(
        functools.partial(interleave_kernel, width, parts, split),
        out_shape=(jax.ShapeDtypeStruct(out, dtype),) * groups if split else (jax.ShapeDtypeStruct(whole, dtype),),
        in_specs=[SMEM, HBM, HBM],
        out_specs=(HBM,) * (groups if split else 1),
        scratch_shapes=[
            pltpu.VMEM((rows, cols), dtype),
            pltpu.VMEM((rows, cols), dtype),
            pltpu.VMEM(whole, dtype),
            pltpu.SemaphoreType.DMA((4,)),
            pltpu.SemaphoreType.DMA((groups,)),
        ],
        compiler_params=pltpu.CompilerParams(vmem_limit_bytes=58 * 2**20),
        name="interleave",
    )(place, *arrays)


def group_at(place_ref, j, width):
    return pl.multiple_of((place_ref[1] ^ j) * width, HEAD_DIM)


def spread_kernel(place_ref, x_ref, *refs):
    *pieces, a_ref, b_ref = refs
    groups, _, width = x_ref.shape
    half = width // 2
    for g in range(groups):
        a_ref[:, g * width : g * width + half] = x_ref[g, :, :half]
        b_ref[:, g * width : g * width + half] = x_ref[g, :, half:]
        cols = pl.ds(group_at(place_ref, g, width) + half, half)
        a_ref[:, cols] = pieces[g][:, :half]
        b_ref[:, cols] = pieces[g][:, half:]


def spread(place, x, pieces):
    groups, rows, width = x.shape
    shape = jax.ShapeDtypeStruct((rows, groups * width), x.dtype)
    return pl.pallas_call(
        spread_kernel,
        out_shape=(shape, shape),
        in_specs=[SMEM] + [VMEM] * (groups + 1),
        out_specs=(VMEM, VMEM),
        compiler_params=pltpu.CompilerParams(vmem_limit_bytes=16 * 2**20),
        name="spread",
    )(place, x, *pieces)


def add_kernel(place_ref, own0_ref, own1_ref, back0_ref, back1_ref, *out_refs):
    rows = out_refs[0].shape[0]
    for j, out_ref in enumerate(out_refs):
        at = pl.ds(group_at(place_ref, j, rows), rows)
        for h, (own, back) in enumerate(((own0_ref, back0_ref), (own1_ref, back1_ref))):
            for n, scale in enumerate((SCORE_SCALE, 1.0)):
                total = (own[n, :, at] * scale).T + back[at, n * HEAD_DIM : (n + 1) * HEAD_DIM].astype(jnp.float32)
                cols = slice((2 * n + h) * HEAD_DIM, (2 * n + h + 1) * HEAD_DIM)
                out_ref[:, cols] = total.astype(jnp.bfloat16)


def add(place, own, back, groups):
    rows, width = back[0].shape
    shape = jax.ShapeDtypeStruct((rows // groups, 2 * width), jnp.bfloat16)
    return pl.pallas_call(
        add_kernel,
        out_shape=(shape,) * groups,
        in_specs=[SMEM] + [VMEM] * 4,
        out_specs=(VMEM,) * groups,
        compiler_params=pltpu.CompilerParams(vmem_limit_bytes=16 * 2**20),
        name="add",
    )(place, *own, *back)


def unpack_kernel(place_ref, *refs):
    *pieces, a_ref, b_ref = refs
    half = pieces[0].shape[1] // 2
    for j, piece in enumerate(pieces):
        cols = pl.ds(group_at(place_ref, j, half), half)
        a_ref[:, cols] = piece[:, :half]
        b_ref[:, cols] = piece[:, half:]


def unpack(place, pieces):
    rows, width = pieces[0].shape
    shape = jax.ShapeDtypeStruct((rows, len(pieces) * width // 2), pieces[0].dtype)
    return pl.pallas_call(
        unpack_kernel,
        out_shape=(shape, shape),
        in_specs=[SMEM] + [VMEM] * len(pieces),
        out_specs=(VMEM, VMEM),
        compiler_params=pltpu.CompilerParams(vmem_limit_bytes=16 * 2**20),
        name="unpack",
    )(place, *pieces)


def body(queries, key_rows, value_rows, grad_out):
    shards, split = lax.axis_size("seq"), lax.axis_size("kvh")
    rows = queries.shape[0]
    apart = WINDOW // (rows * split)
    members = apart * split
    heads = key_rows.shape[1] // (members * HEAD_DIM)
    groups = [[g * members + i for i in range(members)] for g in range(shards // apart)]
    spot = lax.axis_index(("seq", "kvh"))
    place = jnp.stack([lax.axis_index("seq") < apart, spot % members]).astype(jnp.int32)

    def exchange(x):
        return lax.all_to_all(x, ("seq", "kvh"), 0, 0, tiled=True, axis_index_groups=groups)

    def swap(pieces):
        every = range(shards * split)
        out = [pieces[0]] * members
        order = sorted(range(1, members), key=lambda j: j == 1)
        for n, j in enumerate(order):
            piece = pieces[j]
            if n >= IN_FLIGHT:
                before = order[n - IN_FLIGHT]
                piece, out[before] = lax.optimization_barrier((piece, out[before]))
            out[j] = lax.ppermute(piece, ("seq", "kvh"), [(i, i ^ j) for i in every])
        return out

    def onward(x):
        return lax.ppermute(x, "seq", [(i, i + apart) for i in range(shards - apart)])

    def backward(x):
        return lax.ppermute(x, "seq", [(i + apart, i) for i in range(shards - apart)])

    stride = heads * HEAD_DIM
    kv_parts = [(n, h * HEAD_DIM, stride) for h in range(heads) for n in range(2)]
    (own,) = interleave(place, (key_rows, value_rows), members, HEAD_DIM, kv_parts)
    own = exchange(own).reshape(WINDOW, -1)
    halos = [onward(own[:, h * PAIR : (h + 1) * PAIR]) for h in range(heads)]
    outs, down, back = [], [], []
    for h in range(heads):
        qo_parts = [(n, h * PAIR, 2 * stride) for n in range(2)]
        (qo,) = interleave(place, (queries, grad_out), members, PAIR, qo_parts)
        qo = exchange(qo).reshape(WINDOW, -1)
        last = h == heads - 1
        *ao, dhalo, mine = attention(h, place, qo, halos[h], own, members if last else 1)
        if h > 0:
            ao, back[h - 1] = lax.optimization_barrier((ao, back[h - 1]))
        back.append(backward(dhalo))
        outs.append(swap(ao) if last else exchange(ao[0].reshape(members, rows, -1)))
        down.append(mine)
    total = add(place, down, back, members)
    outs[-1], total = lax.optimization_barrier((outs[-1], total))
    grad_k, grad_v = unpack(place, swap(total))
    attended, grad_q = spread(place, *outs)
    return (attended, grad_q, grad_k, grad_v)


def solution(mesh):
    placed = P(("seq", "kvh"), None)
    return jax.shard_map(
        body, mesh=mesh, in_specs=(placed,) * 4, out_specs=(placed,) * 4, check_vma=False
    )
```

```python
import functools

import jax
import jax.numpy as jnp
from jax import lax
from jax.experimental import pallas as pl
from jax.experimental.pallas import tpu as pltpu
from jax.sharding import PartitionSpec as P

HEAD_DIM = 128
PAIR = 2 * HEAD_DIM
WINDOW = 1024
BLOCK = 128
CHUNKS = WINDOW // BLOCK + 1
SCORE_SCALE = 168.0 ** (-0.5)
EXP2_SCALE = SCORE_SCALE * 1.4426950408889634
EXCLUDED = -1e30
ONES = 16
IN_FLIGHT = 4
HOLD = 3
EARLY = 4

NN = (((1,), (0,)), ((), ()))
NT = (((1,), (1,)), ((), ()))

VMEM = pl.BlockSpec(memory_space=pltpu.VMEM)
SMEM = pl.BlockSpec(memory_space=pltpu.SMEM)
ANY = pl.BlockSpec(memory_space=pl.ANY)
HBM = pl.BlockSpec(memory_space=pltpu.HBM)


def dot(left, right, dims):
    return lax.dot_general(left, right, dims, preferred_element_type=jnp.float32)


def side_by_side(x):
    return jnp.concatenate([x[:, :HEAD_DIM].T, x[:, HEAD_DIM:].T], 1)


def attention_kernel(
    taken, pieces, place_ref, *refs
):
    qo_hbm, (halo_hbm, own_hbm, *refs) = refs[:taken], refs[taken:]
    ao_hbm, (dhalo_hbm, down_hbm, *refs) = refs[:pieces], refs[pieces:]
    (kv, qo, ao, dhalo, keys_t, values_t, acc_k, acc_v, exps0, exps1, q_turned, o_turned, in_sem, q_sem, out_sem) = refs
    rows = qo.shape[0]
    blocks = rows // BLOCK
    whole = WINDOW // BLOCK
    exps = (exps0, exps1)

    def at(i):
        return pl.ds(pl.multiple_of(i * BLOCK, BLOCK), BLOCK)

    def span(i):
        return pl.ds(pl.multiple_of(i * BLOCK, BLOCK), CHUNKS * BLOCK)

    def qo_copy(i, piece=0):
        source = qo_hbm[0].at[at(i)] if taken == 1 else qo_hbm[piece]
        return pltpu.make_async_copy(source, qo.at[at(i)], q_sem.at[i])

    def ao_copy(i):
        return pltpu.make_async_copy(ao.at[at(i)], ao_hbm[0].at[at(i)], out_sem.at[0, i])

    def piece_copy(j):
        return pltpu.make_async_copy(ao.at[at(place_ref[1] ^ j)], ao_hbm[j], out_sem.at[0, j])

    def dhalo_copy(i):
        return pltpu.make_async_copy(dhalo.at[at(i)], dhalo_hbm.at[at(i)], out_sem.at[1, i])

    halo_copy = pltpu.make_async_copy(halo_hbm, kv.at[pl.ds(0, WINDOW)], in_sem.at[0])
    own_copy = pltpu.make_async_copy(own_hbm, kv.at[pl.ds(WINDOW, rows)], in_sem.at[1])
    halo_copy.start()
    own_copy.start()
    for i in range(blocks):
        (qo_copy(i) if taken == 1 else qo_copy(place_ref[1] ^ i, i)).start()

    ones_row = lax.broadcasted_iota(jnp.int32, (ONES, values_t.shape[1]), 0) == 0
    values_t[HEAD_DIM:, :] = jnp.where(ones_row, 1.0, 0.0).astype(jnp.bfloat16)
    acc_k[:, : WINDOW + BLOCK] = jnp.zeros((HEAD_DIM, WINDOW + BLOCK), jnp.float32)
    acc_v[:, : WINDOW + BLOCK] = jnp.zeros((HEAD_DIM, WINDOW + BLOCK), jnp.float32)
    exps1[...] = jnp.ones_like(exps1)
    q_turned[...] = jnp.zeros_like(q_turned)
    o_turned[...] = jnp.zeros_like(o_turned)
    key_at = lax.broadcasted_iota(jnp.int32, (BLOCK, 2 * BLOCK), 0)
    query_at = lax.broadcasted_iota(jnp.int32, (BLOCK, 2 * BLOCK), 1) & (BLOCK - 1)
    first = place_ref[0]

    def turn(target, source):
        keys_t[:, at(target)] = kv[at(source), :HEAD_DIM].T
        values_t[:HEAD_DIM, at(target)] = kv[at(source), HEAD_DIM:].T

    halo_copy.wait()
    own_copy.wait()
    for c in range(whole + 1):
        turn(c, c)

    def scores_of(slot, i):
        q_t, o_t = side_by_side(qo[at(i), :PAIR]), side_by_side(qo[at(i), PAIR:])
        q_turned[slot] = q_t
        o_turned[slot] = o_t
        bias = [
            jnp.where((first > 0) & (i + c < whole), EXCLUDED, 0.0).astype(jnp.float32) for c in range(CHUNKS - 1)
        ]
        scores = dot(kv[span(i), :HEAD_DIM], q_t, NN)
        parts = [scores[c * BLOCK : (c + 1) * BLOCK] for c in range(CHUNKS)]
        parts[0] = jnp.where(key_at > query_at, parts[0], EXCLUDED)
        parts[-1] = jnp.where(key_at <= query_at, parts[-1], EXCLUDED)
        top = jnp.max(parts[-1], axis=0, keepdims=True)
        for c in range(CHUNKS - 1):
            top = jnp.maximum(top, jnp.max(parts[c], axis=0, keepdims=True) + bias[c])
        top = top * EXP2_SCALE
        return parts, [top - b for b in bias] + [top]

    def exponentials(slot, parts, shifts):
        for c in range(CHUNKS):
            exps[slot][c * BLOCK : (c + 1) * BLOCK] = jnp.exp2(parts[c] * EXP2_SCALE - shifts[c]).astype(jnp.bfloat16)

    def attended_of(slot, i):
        out = dot(values_t[:, span(i)], exps[slot][...], NN)
        inverse = 1.0 / out[HEAD_DIM : HEAD_DIM + 1]
        out = out[:HEAD_DIM] * inverse
        grad_out = o_turned[slot].astype(jnp.float32)
        delta = jnp.sum(out * grad_out, axis=0, keepdims=True)
        out = out.astype(jnp.bfloat16)
        ao[at(i), :HEAD_DIM] = out[:, :BLOCK].T
        ao[at(i), HEAD_DIM:PAIR] = out[:, BLOCK:].T
        o_scaled = (grad_out * inverse).astype(jnp.bfloat16)
        q_scaled = (q_turned[slot].astype(jnp.float32) * inverse).astype(jnp.bfloat16)
        return inverse, delta, o_scaled, q_scaled

    def gradients(slot, i, inverse, delta, o_scaled, q_scaled):
        grad_weights = dot(kv[span(i), HEAD_DIM:], o_turned[slot], NN)
        grad_scores = []
        for c in range(CHUNKS):
            part = slice(c * BLOCK, (c + 1) * BLOCK)
            grad_scores.append(
                (exps[slot][part].astype(jnp.float32) * (grad_weights[part] - delta)).astype(jnp.bfloat16)
            )
        grad_scores = jnp.concatenate(grad_scores, 0)
        acc_v[:, span(i)] += dot(o_scaled, exps[slot][...], NT)
        grad_q = (dot(keys_t[:, span(i)], grad_scores, NN) * (inverse * SCORE_SCALE)).astype(jnp.bfloat16)
        ao[at(i), PAIR : PAIR + HEAD_DIM] = grad_q[:, :BLOCK].T
        ao[at(i), PAIR + HEAD_DIM :] = grad_q[:, BLOCK:].T
        acc_k[:, span(i)] += dot(q_scaled, grad_scores, NT)

    def flush(i):
        dhalo[at(i), :HEAD_DIM] = (acc_k[:, at(i)] * SCORE_SCALE).astype(jnp.bfloat16).T
        dhalo[at(i), HEAD_DIM:] = acc_v[:, at(i)].astype(jnp.bfloat16).T

    def both(slot, i, before):
        known = attended_of(1 - slot, before)
        parts, shifts = scores_of(slot, i)
        exponentials(slot, parts, shifts)
        gradients(1 - slot, before, *known)
        flush(before)
        turn(i + whole + 1, jnp.minimum(i + whole + 1, whole + blocks - 1))
        acc_k[:, at(i + whole + 1)] = jnp.zeros((HEAD_DIM, BLOCK), jnp.float32)
        acc_v[:, at(i + whole + 1)] = jnp.zeros((HEAD_DIM, BLOCK), jnp.float32)

    def step(j, carry):
        i = 2 * j
        qo_copy(i).wait()
        qo_copy(i + 1).wait()
        both(0, i, jnp.maximum(i - 1, 0))
        both(1, i + 1, i)

        @pl.when(j > 0)
        def _():
            if pieces == 1:
                ao_copy(i - 1).start()
            dhalo_copy(i - 1).start()

        if pieces == 1:
            ao_copy(i).start()
        dhalo_copy(i).start()
        return carry

    lax.fori_loop(0, blocks // 2, step, 0)
    gradients(1, blocks - 1, *attended_of(1, blocks - 1))
    flush(blocks - 1)
    dhalo_copy(blocks - 1).start()
    if pieces == 1:
        ao_copy(blocks - 1).start()
    else:
        for j in range(pieces):
            piece_copy(j).start()
    own_k = pltpu.make_async_copy(acc_k.at[:, pl.ds(WINDOW, rows)], down_hbm.at[0], in_sem.at[0])
    own_v = pltpu.make_async_copy(acc_v.at[:, pl.ds(WINDOW, rows)], down_hbm.at[1], in_sem.at[1])
    own_k.start()
    own_v.start()
    for i in range(blocks):
        (ao_copy(i) if pieces == 1 else piece_copy(i)).wait()
        dhalo_copy(i).wait()
    own_k.wait()
    own_v.wait()


def attention(place, qo, halo, own, pieces):
    rows = own.shape[0]
    blocks = rows // BLOCK
    reach = WINDOW + rows
    bf16, f32 = jnp.bfloat16, jnp.float32
    return pl.pallas_call(
        functools.partial(attention_kernel, len(qo), pieces),
        out_shape=(
            *[jax.ShapeDtypeStruct((rows // pieces, 2 * PAIR), bf16)] * pieces,
            jax.ShapeDtypeStruct(halo.shape, bf16),
            jax.ShapeDtypeStruct((2, HEAD_DIM, rows), f32),
        ),
        in_specs=[SMEM] + [ANY] * (len(qo) + 2),
        out_specs=(HBM,) * (pieces + 2),
        scratch_shapes=[
            pltpu.VMEM((reach, PAIR), bf16),
            pltpu.VMEM((rows, 2 * PAIR), bf16),
            pltpu.VMEM((rows, 2 * PAIR), bf16),
            pltpu.VMEM(halo.shape, bf16),
            pltpu.VMEM((HEAD_DIM, reach + BLOCK), bf16),
            pltpu.VMEM((HEAD_DIM + ONES, reach + BLOCK), bf16),
            pltpu.VMEM((HEAD_DIM, reach + BLOCK), f32),
            pltpu.VMEM((HEAD_DIM, reach + BLOCK), f32),
            pltpu.VMEM((CHUNKS * BLOCK, 2 * BLOCK), bf16),
            pltpu.VMEM((CHUNKS * BLOCK, 2 * BLOCK), bf16),
            pltpu.VMEM((2, HEAD_DIM, 2 * BLOCK), bf16),
            pltpu.VMEM((2, HEAD_DIM, 2 * BLOCK), bf16),
            pltpu.SemaphoreType.DMA((2,)),
            pltpu.SemaphoreType.DMA((blocks,)),
            pltpu.SemaphoreType.DMA((2, blocks)),
        ],
        compiler_params=pltpu.CompilerParams(vmem_limit_bytes=58 * 2**20),
        cost_estimate=pl.CostEstimate(flops=10**10, bytes_accessed=4 * 2**20, transcendentals=0),
        name="attention",
    )(place, *qo, halo, own)


def interleave_kernel(width, sets, place_ref, *refs):
    arrays, refs = refs[:2], refs[2:]
    groups = arrays[0].shape[1] // sets[0][1][0][2]
    outs, refs = refs[: -(4 + len(sets))], refs[-(4 + len(sets)) :]
    fetched, staged, (in_sem, out_sem) = refs[:2], refs[2:-2], refs[-2:]
    loads = [pltpu.make_async_copy(arrays[n], fetched[n], in_sem.at[n]) for n in range(2)]
    for load in loads:
        load.start()
    for load in loads:
        load.wait()
    stores = []
    taken = 0
    for k, (split, parts) in enumerate(sets):
        for g in range(groups):
            source = place_ref[1] ^ g if split else g
            for n, (which, start, stride) in enumerate(parts):
                at = source * stride + start
                if split:
                    at = pl.multiple_of(at, HEAD_DIM)
                staged[k][g, :, n * width : (n + 1) * width] = fetched[which][:, pl.ds(at, width)]
            out = outs[taken + g] if split else outs[taken].at[g]
            stores.append(pltpu.make_async_copy(staged[k].at[g], out, out_sem.at[k, g]))
            stores[-1].start()
        taken += groups if split else 1
    for store in stores:
        store.wait()


def interleave(place, arrays, groups, width, sets):
    rows, cols = arrays[0].shape
    dtype = arrays[0].dtype
    shapes, staged = [], []
    for split, parts in sets:
        whole = (groups, rows, width * len(parts))
        staged.append(pltpu.VMEM(whole, dtype))
        shapes += [jax.ShapeDtypeStruct(whole[1:], dtype)] * groups if split else [jax.ShapeDtypeStruct(whole, dtype)]
    return pl.pallas_call(
        functools.partial(interleave_kernel, width, sets),
        out_shape=tuple(shapes),
        in_specs=[SMEM, HBM, HBM],
        out_specs=(HBM,) * len(shapes),
        scratch_shapes=[
            pltpu.VMEM((rows, cols), dtype),
            pltpu.VMEM((rows, cols), dtype),
            *staged,
            pltpu.SemaphoreType.DMA((2,)),
            pltpu.SemaphoreType.DMA((len(sets), groups)),
        ],
        compiler_params=pltpu.CompilerParams(vmem_limit_bytes=58 * 2**20),
        name="interleave",
    )(place, *arrays)


def assemble_kernel(place_ref, *refs):
    *arrays, sem = refs
    count, heads = sem.shape
    pieces, outs = arrays[:count], arrays[count:]
    rows, width = pieces[0].shape[0], outs[0].shape[1]
    copies = []
    for j in range(count):
        at = pl.ds(pl.multiple_of((place_ref[1] ^ j) * rows, BLOCK), rows)
        for h in range(heads):
            source = pieces[j].at[:, pl.ds(h * width, width)]
            copies.append(pltpu.make_async_copy(source, outs[h].at[at], sem.at[j, h]))
    for copy in copies:
        copy.start()
    for copy in copies:
        copy.wait()


def assemble(place, pieces, heads):
    rows, width = pieces[0].shape
    shape = jax.ShapeDtypeStruct((len(pieces) * rows, width // heads), pieces[0].dtype)
    return pl.pallas_call(
        assemble_kernel,
        out_shape=(shape,) * heads,
        in_specs=[SMEM] + [ANY] * len(pieces),
        out_specs=(VMEM,) * heads,
        scratch_shapes=[pltpu.SemaphoreType.DMA((len(pieces), heads))],
        compiler_params=pltpu.CompilerParams(vmem_limit_bytes=8 * 2**20),
        name="assemble",
    )(place, *pieces)


def group_at(place_ref, j, width):
    return pl.multiple_of((place_ref[1] ^ j) * width, HEAD_DIM)


def spread_kernel(place_ref, x_ref, *refs):
    *pieces, a_ref, b_ref = refs
    groups, _, width = x_ref.shape
    half = width // 2
    for g in range(groups):
        a_ref[:, g * width : g * width + half] = x_ref[g, :, :half]
        b_ref[:, g * width : g * width + half] = x_ref[g, :, half:]
        cols = pl.ds(group_at(place_ref, g, width) + half, half)
        a_ref[:, cols] = pieces[g][:, :half]
        b_ref[:, cols] = pieces[g][:, half:]


def spread(place, x, pieces):
    groups, rows, width = x.shape
    shape = jax.ShapeDtypeStruct((rows, groups * width), x.dtype)
    return pl.pallas_call(
        spread_kernel,
        out_shape=(shape, shape),
        in_specs=[SMEM] + [VMEM] * (groups + 1),
        out_specs=(VMEM, VMEM),
        compiler_params=pltpu.CompilerParams(vmem_limit_bytes=16 * 2**20),
        name="spread",
    )(place, x, *pieces)


def add_kernel(place_ref, own0_ref, own1_ref, back0_ref, back1_ref, *out_refs):
    rows = out_refs[0].shape[0]
    for j, out_ref in enumerate(out_refs):
        at = pl.ds(group_at(place_ref, j, rows), rows)
        for h, (own, back) in enumerate(((own0_ref, back0_ref), (own1_ref, back1_ref))):
            for n, scale in enumerate((SCORE_SCALE, 1.0)):
                total = (own[n, :, at] * scale).T + back[at, n * HEAD_DIM : (n + 1) * HEAD_DIM].astype(jnp.float32)
                cols = slice((2 * n + h) * HEAD_DIM, (2 * n + h + 1) * HEAD_DIM)
                out_ref[:, cols] = total.astype(jnp.bfloat16)


def add(place, own, back, groups):
    rows, width = back[0].shape
    shape = jax.ShapeDtypeStruct((rows // groups, 2 * width), jnp.bfloat16)
    return pl.pallas_call(
        add_kernel,
        out_shape=(shape,) * groups,
        in_specs=[SMEM] + [VMEM] * 4,
        out_specs=(VMEM,) * groups,
        compiler_params=pltpu.CompilerParams(vmem_limit_bytes=16 * 2**20),
        name="add",
    )(place, *own, *back)


def unpack_kernel(place_ref, *refs):
    *pieces, a_ref, b_ref = refs
    half = pieces[0].shape[1] // 2
    for j, piece in enumerate(pieces):
        cols = pl.ds(group_at(place_ref, j, half), half)
        a_ref[:, cols] = piece[:, :half]
        b_ref[:, cols] = piece[:, half:]


def unpack(place, pieces):
    rows, width = pieces[0].shape
    shape = jax.ShapeDtypeStruct((rows, len(pieces) * width // 2), pieces[0].dtype)
    return pl.pallas_call(
        unpack_kernel,
        out_shape=(shape, shape),
        in_specs=[SMEM] + [VMEM] * len(pieces),
        out_specs=(VMEM, VMEM),
        compiler_params=pltpu.CompilerParams(vmem_limit_bytes=16 * 2**20),
        name="unpack",
    )(place, *pieces)


def body(queries, key_rows, value_rows, grad_out):
    shards, split = lax.axis_size("seq"), lax.axis_size("kvh")
    rows = queries.shape[0]
    apart = WINDOW // (rows * split)
    members = apart * split
    heads = key_rows.shape[1] // (members * HEAD_DIM)
    groups = [[g * members + i for i in range(members)] for g in range(shards // apart)]
    spot = lax.axis_index(("seq", "kvh"))
    place = jnp.stack([lax.axis_index("seq") < apart, spot % members]).astype(jnp.int32)

    def exchange(x):
        return lax.all_to_all(x, ("seq", "kvh"), 0, 0, tiled=True, axis_index_groups=groups)

    order = sorted(range(1, members), key=lambda j: j == 1)

    def swap(pieces, before=None, limit=IN_FLIGHT):
        every = range(shards * split)
        out = [pieces[0]] * members
        sent = [] if before is None else [(before, j) for j in order]
        for j in order:
            piece = pieces[j]
            if len(sent) >= limit:
                box, k = sent[-limit]
                piece, box[k] = lax.optimization_barrier((piece, box[k]))
            out[j] = lax.ppermute(piece, ("seq", "kvh"), [(i, i ^ j) for i in every])
            sent.append((out, j))
        return out

    def onward(x):
        return lax.ppermute(x, "seq", [(i, (i + apart) % shards) for i in range(shards)])

    def backward(x):
        return lax.ppermute(x, "seq", [((i + apart) % shards, i) for i in range(shards)])

    stride = heads * HEAD_DIM
    kv_parts = [(n, h * HEAD_DIM, stride) for h in range(heads) for n in range(2)]
    def qo_parts(h):
        return [(n, h * PAIR, 2 * stride) for n in range(2)]

    kv = list(interleave(place, (key_rows, value_rows), members, HEAD_DIM, [(True, kv_parts)]))
    sets = [(h == 0, qo_parts(h)) for h in range(heads)]
    packed = interleave(place, (queries, grad_out), members, PAIR, sets)
    late = order[EARLY]
    kv[late], (*first, second) = lax.optimization_barrier((kv[late], packed))
    kv = swap(kv, None, 5)
    first = swap(first, kv, 5)
    own = assemble(place, kv, heads)
    second, first[order[HOLD]] = lax.optimization_barrier((second, first[order[HOLD]]))
    qos = [first, [exchange(second).reshape(WINDOW, -1)]]
    held, first[order[-2]] = lax.optimization_barrier((own[1], first[order[-2]]))
    halos = [onward(own[0]), onward(held)]
    outs, down, back = [], [], []
    for h in range(heads):
        last = h == heads - 1
        *ao, dhalo, mine = attention(place, qos[h], halos[h], own[h], members if last else 1)
        if h > 0:
            ao, back[h - 1] = lax.optimization_barrier((ao, back[h - 1]))
        back.append(backward(dhalo))
        outs.append(swap(ao) if last else exchange(ao[0].reshape(members, rows, -1)))
        down.append(mine)
    total = add(place, down, back, members)
    outs[-1], total = lax.optimization_barrier((outs[-1], total))
    grad_k, grad_v = unpack(place, swap(total))
    attended, grad_q = spread(place, *outs)
    return (attended, grad_q, grad_k, grad_v)


def solution(mesh):
    placed = P(("seq", "kvh"), None)
    return jax.shard_map(
        body, mesh=mesh, in_specs=(placed,) * 4, out_specs=(placed,) * 4, check_vma=False
    )
```

```python
import functools

import jax
import jax.numpy as jnp
from jax import lax
from jax.experimental import pallas as pl
from jax.experimental.pallas import tpu as pltpu
from jax.sharding import PartitionSpec as P

HEAD_DIM = 128
PAIR = 2 * HEAD_DIM
WINDOW = 1024
BLOCK = 128
CHUNKS = WINDOW // BLOCK + 1
SCORE_SCALE = 168.0 ** (-0.5)
EXP2_SCALE = SCORE_SCALE * 1.4426950408889634
EXCLUDED = -1e30
ONES = 16
IN_FLIGHT = 4
HOLD = 3
EARLY = 4

NN = (((1,), (0,)), ((), ()))
NT = (((1,), (1,)), ((), ()))

VMEM = pl.BlockSpec(memory_space=pltpu.VMEM)
SMEM = pl.BlockSpec(memory_space=pltpu.SMEM)
ANY = pl.BlockSpec(memory_space=pl.ANY)
HBM = pl.BlockSpec(memory_space=pltpu.HBM)


def dot(left, right, dims):
    return lax.dot_general(left, right, dims, preferred_element_type=jnp.float32)


class Place:
    def __init__(self, apart):
        split = lax.axis_size("kvh")
        self.shard = lax.axis_index("seq")
        self.first = self.shard < apart
        self.member = lax.rem(self.shard, apart) * split + lax.axis_index("kvh")


def side_by_side(x):
    return jnp.concatenate([x[:, :HEAD_DIM].T, x[:, HEAD_DIM:].T], 1)


def attention_kernel(
    apart, taken, pieces, joins, *refs
):
    place = Place(apart)
    qo_hbm, (halo_hbm, own_hbm, *refs) = refs[:taken], refs[taken:]
    (mine_hbm, back_hbm), refs = refs[:2] if joins else (None, None), refs[2 * joins :]
    ao_hbm, (dhalo_hbm, down_hbm, *refs) = refs[:pieces], refs[pieces:]
    (kv, qo, ao, dhalo, keys_t, values_t, acc_k, acc_v, exps0, exps1, q_turned, o_turned, mine, back, in_sem, q_sem, out_sem) = refs
    rows = qo.shape[0]
    blocks = rows // BLOCK
    whole = WINDOW // BLOCK
    exps = (exps0, exps1)

    def at(i):
        return pl.ds(pl.multiple_of(i * BLOCK, BLOCK), BLOCK)

    def span(i):
        return pl.ds(pl.multiple_of(i * BLOCK, BLOCK), CHUNKS * BLOCK)

    def qo_copy(i, piece=0):
        source = qo_hbm[0].at[at(i)] if taken == 1 else qo_hbm[piece]
        return pltpu.make_async_copy(source, qo.at[at(i)], q_sem.at[i])

    def ao_copy(i):
        return pltpu.make_async_copy(ao.at[at(i)], ao_hbm[0].at[at(i)], out_sem.at[0, i])

    def piece_copy(j):
        return pltpu.make_async_copy(ao.at[at(place.member ^ j)], ao_hbm[j], out_sem.at[0, j])

    def dhalo_copy(i):
        return pltpu.make_async_copy(dhalo.at[at(i)], dhalo_hbm.at[at(i)], out_sem.at[1, i])

    halo_copy = pltpu.make_async_copy(halo_hbm, kv.at[pl.ds(0, WINDOW)], in_sem.at[0])
    own_copy = pltpu.make_async_copy(own_hbm, kv.at[pl.ds(WINDOW, rows)], in_sem.at[1])
    halo_copy.start()
    own_copy.start()
    if joins:
        mine_copy = pltpu.make_async_copy(mine_hbm, mine, in_sem.at[2])
        back_copy = pltpu.make_async_copy(back_hbm, back, in_sem.at[3])
    for i in range(blocks):
        (qo_copy(i) if taken == 1 else qo_copy(place.member ^ i, i)).start()

    if joins:
        mine_copy.start()
        back_copy.start()

    ones_row = lax.broadcasted_iota(jnp.int32, (ONES, values_t.shape[1]), 0) == 0
    values_t[HEAD_DIM:, :] = jnp.where(ones_row, 1.0, 0.0).astype(jnp.bfloat16)
    acc_k[:, : WINDOW + BLOCK] = jnp.zeros((HEAD_DIM, WINDOW + BLOCK), jnp.float32)
    acc_v[:, : WINDOW + BLOCK] = jnp.zeros((HEAD_DIM, WINDOW + BLOCK), jnp.float32)
    exps1[...] = jnp.ones_like(exps1)
    q_turned[...] = jnp.zeros_like(q_turned)
    o_turned[...] = jnp.zeros_like(o_turned)
    key_at = lax.broadcasted_iota(jnp.int32, (BLOCK, 2 * BLOCK), 0)
    query_at = lax.broadcasted_iota(jnp.int32, (BLOCK, 2 * BLOCK), 1) & (BLOCK - 1)
    first = place.first

    def turn(target, source):
        keys_t[:, at(target)] = kv[at(source), :HEAD_DIM].T
        values_t[:HEAD_DIM, at(target)] = kv[at(source), HEAD_DIM:].T

    halo_copy.wait()
    own_copy.wait()
    if joins:
        mine_copy.wait()
        back_copy.wait()
    for c in range(whole + 1):
        turn(c, c)

    def scores_of(slot, i):
        q_t, o_t = side_by_side(qo[at(i), :PAIR]), side_by_side(qo[at(i), PAIR:])
        q_turned[slot] = q_t
        o_turned[slot] = o_t
        bias = [
            jnp.where(first & (i + c < whole), EXCLUDED, 0.0).astype(jnp.float32) for c in range(CHUNKS - 1)
        ]
        scores = dot(kv[span(i), :HEAD_DIM], q_t, NN)
        parts = [scores[c * BLOCK : (c + 1) * BLOCK] for c in range(CHUNKS)]
        parts[0] = jnp.where(key_at > query_at, parts[0], EXCLUDED)
        parts[-1] = jnp.where(key_at <= query_at, parts[-1], EXCLUDED)
        top = jnp.max(parts[-1], axis=0, keepdims=True)
        for c in range(CHUNKS - 1):
            top = jnp.maximum(top, jnp.max(parts[c], axis=0, keepdims=True) + bias[c])
        top = top * EXP2_SCALE
        return parts, [top - b for b in bias] + [top]

    def exponentials(slot, parts, shifts):
        for c in range(CHUNKS):
            exps[slot][c * BLOCK : (c + 1) * BLOCK] = jnp.exp2(parts[c] * EXP2_SCALE - shifts[c]).astype(jnp.bfloat16)

    def attended_of(slot, i):
        out = dot(values_t[:, span(i)], exps[slot][...], NN)
        inverse = 1.0 / out[HEAD_DIM : HEAD_DIM + 1]
        out = out[:HEAD_DIM] * inverse
        grad_out = o_turned[slot].astype(jnp.float32)
        delta = jnp.sum(out * grad_out, axis=0, keepdims=True)
        out = out.astype(jnp.bfloat16)
        ao[at(i), :HEAD_DIM] = out[:, :BLOCK].T
        ao[at(i), HEAD_DIM:PAIR] = out[:, BLOCK:].T
        o_scaled = (grad_out * inverse).astype(jnp.bfloat16)
        q_scaled = (q_turned[slot].astype(jnp.float32) * inverse).astype(jnp.bfloat16)
        return inverse, delta, o_scaled, q_scaled

    def gradients(slot, i, inverse, delta, o_scaled, q_scaled):
        grad_weights = dot(kv[span(i), HEAD_DIM:], o_turned[slot], NN)
        grad_scores = []
        for c in range(CHUNKS):
            part = slice(c * BLOCK, (c + 1) * BLOCK)
            grad_scores.append(
                (exps[slot][part].astype(jnp.float32) * (grad_weights[part] - delta)).astype(jnp.bfloat16)
            )
        grad_scores = jnp.concatenate(grad_scores, 0)
        acc_v[:, span(i)] += dot(o_scaled, exps[slot][...], NT)
        grad_q = (dot(keys_t[:, span(i)], grad_scores, NN) * (inverse * SCORE_SCALE)).astype(jnp.bfloat16)
        ao[at(i), PAIR : PAIR + HEAD_DIM] = grad_q[:, :BLOCK].T
        ao[at(i), PAIR + HEAD_DIM : 2 * PAIR] = grad_q[:, BLOCK:].T
        acc_k[:, span(i)] += dot(q_scaled, grad_scores, NT)

    def flush(i):
        dhalo[at(i), :HEAD_DIM] = (acc_k[:, at(i)] * SCORE_SCALE).astype(jnp.bfloat16).T
        dhalo[at(i), HEAD_DIM:] = acc_v[:, at(i)].astype(jnp.bfloat16).T

    def join(i):
        for n, scale in enumerate((SCORE_SCALE, 1.0)):
            cols = slice(n * HEAD_DIM, (n + 1) * HEAD_DIM)
            total = (mine[n, :, at(i)] * scale).T + back[at(i), cols].astype(jnp.float32)
            ao[at(i), 2 * PAIR + n * HEAD_DIM : 2 * PAIR + (n + 1) * HEAD_DIM] = total.astype(jnp.bfloat16)

    def both(slot, i, before):
        known = attended_of(1 - slot, before)
        parts, shifts = scores_of(slot, i)
        exponentials(slot, parts, shifts)
        gradients(1 - slot, before, *known)
        flush(before)
        if joins:
            join(i)
        turn(i + whole + 1, jnp.minimum(i + whole + 1, whole + blocks - 1))
        acc_k[:, at(i + whole + 1)] = jnp.zeros((HEAD_DIM, BLOCK), jnp.float32)
        acc_v[:, at(i + whole + 1)] = jnp.zeros((HEAD_DIM, BLOCK), jnp.float32)

    def step(j, carry):
        i = 2 * j
        qo_copy(i).wait()
        qo_copy(i + 1).wait()
        both(0, i, jnp.maximum(i - 1, 0))
        both(1, i + 1, i)

        @pl.when(j > 0)
        def _():
            if pieces == 1:
                ao_copy(i - 1).start()
            dhalo_copy(i - 1).start()

        if pieces == 1:
            ao_copy(i).start()
        dhalo_copy(i).start()
        return carry

    lax.fori_loop(0, blocks // 2, step, 0)
    gradients(1, blocks - 1, *attended_of(1, blocks - 1))
    flush(blocks - 1)
    dhalo_copy(blocks - 1).start()
    if pieces == 1:
        ao_copy(blocks - 1).start()
    else:
        for j in range(pieces):
            piece_copy(j).start()
    own_k = pltpu.make_async_copy(acc_k.at[:, pl.ds(WINDOW, rows)], down_hbm.at[0], in_sem.at[0])
    own_v = pltpu.make_async_copy(acc_v.at[:, pl.ds(WINDOW, rows)], down_hbm.at[1], in_sem.at[1])
    own_k.start()
    own_v.start()
    for i in range(blocks):
        (ao_copy(i) if pieces == 1 else piece_copy(i)).wait()
        dhalo_copy(i).wait()
    own_k.wait()
    own_v.wait()


def attention(apart, qo, halo, own, pieces, joined=()):
    rows = own.shape[0]
    blocks = rows // BLOCK
    reach = WINDOW + rows
    bf16, f32 = jnp.bfloat16, jnp.float32
    width = 2 * PAIR + (PAIR if joined else 0)
    small = (8, HEAD_DIM)
    return pl.pallas_call(
        functools.partial(attention_kernel, apart, len(qo), pieces, len(joined) > 0),
        out_shape=(
            *[jax.ShapeDtypeStruct((rows // pieces, width), bf16)] * pieces,
            jax.ShapeDtypeStruct(halo.shape, bf16),
            jax.ShapeDtypeStruct((2, HEAD_DIM, rows), f32),
        ),
        in_specs=[ANY] * (len(qo) + 2 + len(joined)),
        out_specs=(HBM,) * (pieces + 2),
        scratch_shapes=[
            pltpu.VMEM((reach, PAIR), bf16),
            pltpu.VMEM((rows, 2 * PAIR), bf16),
            pltpu.VMEM((rows, width), bf16),
            pltpu.VMEM(halo.shape, bf16),
            pltpu.VMEM((HEAD_DIM, reach + BLOCK), bf16),
            pltpu.VMEM((HEAD_DIM + ONES, reach + BLOCK), bf16),
            pltpu.VMEM((HEAD_DIM, reach + BLOCK), f32),
            pltpu.VMEM((HEAD_DIM, reach + BLOCK), f32),
            pltpu.VMEM((CHUNKS * BLOCK, 2 * BLOCK), bf16),
            pltpu.VMEM((CHUNKS * BLOCK, 2 * BLOCK), bf16),
            pltpu.VMEM((2, HEAD_DIM, 2 * BLOCK), bf16),
            pltpu.VMEM((2, HEAD_DIM, 2 * BLOCK), bf16),
            pltpu.VMEM((2, HEAD_DIM, rows) if joined else small, f32),
            pltpu.VMEM((rows, PAIR) if joined else small, bf16),
            pltpu.SemaphoreType.DMA((4,)),
            pltpu.SemaphoreType.DMA((blocks,)),
            pltpu.SemaphoreType.DMA((2, blocks)),
        ],
        compiler_params=pltpu.CompilerParams(vmem_limit_bytes=58 * 2**20),
        cost_estimate=pl.CostEstimate(flops=10**10, bytes_accessed=4 * 2**20, transcendentals=0),
        name="attention",
    )(*qo, halo, own, *joined)


def interleave_kernel(apart, width, sets, *refs):
    place = Place(apart)
    arrays, refs = refs[:2], refs[2:]
    groups = arrays[0].shape[1] // sets[0][1][0][2]
    outs, refs = refs[: -(4 + len(sets))], refs[-(4 + len(sets)) :]
    fetched, staged, (in_sem, out_sem) = refs[:2], refs[2:-2], refs[-2:]
    loads = [pltpu.make_async_copy(arrays[n], fetched[n], in_sem.at[n]) for n in range(2)]
    for load in loads:
        load.start()
    for load in loads:
        load.wait()
    stores = []
    taken = 0
    for k, (split, parts) in enumerate(sets):
        for g in range(groups):
            source = place.member ^ g if split else g
            for n, (which, start, stride) in enumerate(parts):
                at = source * stride + start
                if split:
                    at = pl.multiple_of(at, HEAD_DIM)
                staged[k][g, :, n * width : (n + 1) * width] = fetched[which][:, pl.ds(at, width)]
            out = outs[taken + g] if split else outs[taken].at[g]
            stores.append(pltpu.make_async_copy(staged[k].at[g], out, out_sem.at[k, g]))
            stores[-1].start()
        taken += groups if split else 1
    for store in stores:
        store.wait()


def interleave(apart, arrays, groups, width, sets):
    rows, cols = arrays[0].shape
    dtype = arrays[0].dtype
    shapes, staged = [], []
    for split, parts in sets:
        whole = (groups, rows, width * len(parts))
        staged.append(pltpu.VMEM(whole, dtype))
        shapes += [jax.ShapeDtypeStruct(whole[1:], dtype)] * groups if split else [jax.ShapeDtypeStruct(whole, dtype)]
    return pl.pallas_call(
        functools.partial(interleave_kernel, apart, width, sets),
        out_shape=tuple(shapes),
        in_specs=[HBM, HBM],
        out_specs=(HBM,) * len(shapes),
        scratch_shapes=[
            pltpu.VMEM((rows, cols), dtype),
            pltpu.VMEM((rows, cols), dtype),
            *staged,
            pltpu.SemaphoreType.DMA((2,)),
            pltpu.SemaphoreType.DMA((len(sets), groups)),
        ],
        compiler_params=pltpu.CompilerParams(vmem_limit_bytes=58 * 2**20),
        name="interleave",
    )(*arrays)


def assemble_kernel(apart, *refs):
    place = Place(apart)
    *arrays, sem = refs
    count, heads = sem.shape
    pieces, outs = arrays[:count], arrays[count:]
    rows, width = pieces[0].shape[0], outs[0].shape[1]
    copies = []
    for j in range(count):
        at = pl.ds(pl.multiple_of((place.member ^ j) * rows, BLOCK), rows)
        for h in range(heads):
            source = pieces[j].at[:, pl.ds(h * width, width)]
            copies.append(pltpu.make_async_copy(source, outs[h].at[at], sem.at[j, h]))
    for copy in copies:
        copy.start()
    for copy in copies:
        copy.wait()


def assemble(apart, pieces, heads):
    rows, width = pieces[0].shape
    shape = jax.ShapeDtypeStruct((len(pieces) * rows, width // heads), pieces[0].dtype)
    return pl.pallas_call(
        functools.partial(assemble_kernel, apart),
        out_shape=(shape,) * heads,
        in_specs=[ANY] * len(pieces),
        out_specs=(VMEM,) * heads,
        scratch_shapes=[pltpu.SemaphoreType.DMA((len(pieces), heads))],
        compiler_params=pltpu.CompilerParams(vmem_limit_bytes=8 * 2**20),
        name="assemble",
    )(*pieces)


def group_at(place, j, width):
    return pl.multiple_of((place.member ^ j) * width, HEAD_DIM)


def spread_kernel(apart, x_ref, *refs):
    place = Place(apart)
    *pieces, a_ref, b_ref = refs
    groups, _, width = x_ref.shape
    half = width // 2
    for g in range(groups):
        a_ref[:, g * width : g * width + half] = x_ref[g, :, :half]
        b_ref[:, g * width : g * width + half] = x_ref[g, :, half:]
        cols = pl.ds(group_at(place, g, width) + half, half)
        a_ref[:, cols] = pieces[g][:, :half]
        b_ref[:, cols] = pieces[g][:, half:]


def spread(apart, x, pieces):
    groups, rows, width = x.shape
    shape = jax.ShapeDtypeStruct((rows, groups * width), x.dtype)
    return pl.pallas_call(
        functools.partial(spread_kernel, apart),
        out_shape=(shape, shape),
        in_specs=[VMEM] * (groups + 1),
        out_specs=(VMEM, VMEM),
        compiler_params=pltpu.CompilerParams(vmem_limit_bytes=16 * 2**20),
        name="spread",
    )(x, *pieces)


def settle_kernel(own0, own1, back0, done_ref, open_ref):
    for n, scale in enumerate((SCORE_SCALE, 1.0)):
        cols = slice(n * HEAD_DIM, (n + 1) * HEAD_DIM)
        for i in range(done_ref.shape[0] // BLOCK):
            at = slice(i * BLOCK, (i + 1) * BLOCK)
            total = (own0[n, :, at] * scale).T + back0[at, cols].astype(jnp.float32)
            done_ref[at, cols] = total.astype(jnp.bfloat16)
            open_ref[at, cols] = (own1[n, :, at] * scale).T


def settle(own, back):
    return pl.pallas_call(
        settle_kernel,
        out_shape=(
            jax.ShapeDtypeStruct(back.shape, jnp.bfloat16),
            jax.ShapeDtypeStruct(back.shape, jnp.float32),
        ),
        in_specs=[VMEM] * 3,
        out_specs=(VMEM,) * 2,
        compiler_params=pltpu.CompilerParams(vmem_limit_bytes=16 * 2**20),
        name="settle",
    )(*own, back)


def add_kernel(apart, done_ref, open_ref, back_ref, *out_refs):
    place = Place(apart)
    rows = out_refs[0].shape[0]
    for j, out_ref in enumerate(out_refs):
        at = pl.ds(group_at(place, j, rows), rows)
        out_ref[:, :PAIR] = done_ref[at, :]
        out_ref[:, PAIR:] = (open_ref[at, :] + back_ref[at, :].astype(jnp.float32)).astype(jnp.bfloat16)


def add(apart, done, started, back, groups):
    rows, width = back.shape
    shape = jax.ShapeDtypeStruct((rows // groups, 2 * width), jnp.bfloat16)
    return pl.pallas_call(
        functools.partial(add_kernel, apart),
        out_shape=(shape,) * groups,
        in_specs=[VMEM] * 3,
        out_specs=(VMEM,) * groups,
        compiler_params=pltpu.CompilerParams(vmem_limit_bytes=16 * 2**20),
        name="add",
    )(done, started, back)


def unpack_kernel(apart, *refs):
    place = Place(apart)
    *pieces, a_ref, b_ref = refs
    heads = pieces[0].shape[1] // PAIR
    for j, piece in enumerate(pieces):
        start = group_at(place, j, heads * HEAD_DIM)
        for h in range(heads):
            cols = pl.ds(start + h * HEAD_DIM, HEAD_DIM)
            a_ref[:, cols] = piece[:, h * PAIR : h * PAIR + HEAD_DIM]
            b_ref[:, cols] = piece[:, h * PAIR + HEAD_DIM : (h + 1) * PAIR]


def unpack(apart, pieces):
    rows, width = pieces[0].shape
    shape = jax.ShapeDtypeStruct((rows, len(pieces) * width // 2), pieces[0].dtype)
    return pl.pallas_call(
        functools.partial(unpack_kernel, apart),
        out_shape=(shape, shape),
        in_specs=[VMEM] * len(pieces),
        out_specs=(VMEM, VMEM),
        compiler_params=pltpu.CompilerParams(vmem_limit_bytes=16 * 2**20),
        name="unpack",
    )(*pieces)


def body(queries, key_rows, value_rows, grad_out):
    shards, split = lax.axis_size("seq"), lax.axis_size("kvh")
    rows = queries.shape[0]
    apart = WINDOW // (rows * split)
    members = apart * split
    heads = key_rows.shape[1] // (members * HEAD_DIM)
    groups = [[g * members + i for i in range(members)] for g in range(shards // apart)]
    def exchange(x):
        return lax.all_to_all(x, ("seq", "kvh"), 0, 0, tiled=True, axis_index_groups=groups)

    order = sorted(range(1, members), key=lambda j: j == 1)

    def swap(pieces, before=None, limit=IN_FLIGHT):
        every = range(shards * split)
        out = [pieces[0]] * members
        sent = [] if before is None else [(before, j) for j in order]
        for j in order:
            piece = pieces[j]
            if len(sent) >= limit:
                box, k = sent[-limit]
                piece, box[k] = lax.optimization_barrier((piece, box[k]))
            out[j] = lax.ppermute(piece, ("seq", "kvh"), [(i, i ^ j) for i in every])
            sent.append((out, j))
        return out

    def onward(x):
        return lax.ppermute(x, "seq", [(i, (i + apart) % shards) for i in range(shards)])

    def backward(x):
        return lax.ppermute(x, "seq", [((i + apart) % shards, i) for i in range(shards)])

    stride = heads * HEAD_DIM
    kv_parts = [(n, h * HEAD_DIM, stride) for h in range(heads) for n in range(2)]
    def qo_parts(h):
        return [(n, h * PAIR, 2 * stride) for n in range(2)]

    kv = list(interleave(apart, (key_rows, value_rows), members, HEAD_DIM, [(True, kv_parts)]))
    sets = [(h == 0, qo_parts(h)) for h in range(heads)]
    packed = interleave(apart, (queries, grad_out), members, PAIR, sets)
    late = order[EARLY]
    kv[late], (*first, second) = lax.optimization_barrier((kv[late], packed))
    kv = swap(kv, None, 5)
    first = swap(first, kv, 5)
    own = assemble(apart, kv, heads)
    second, first[order[HOLD]] = lax.optimization_barrier((second, first[order[HOLD]]))
    qos = [first, [exchange(second).reshape(WINDOW, -1)]]
    held, first[order[-2]] = lax.optimization_barrier((own[1], first[order[-2]]))
    halos = [onward(own[0]), onward(held)]
    outs, mine, back = [], [], []
    for h in range(heads):
        last = h == heads - 1
        *ao, dhalo, down = attention(apart, qos[h], halos[h], own[h], members if last else 1)
        if last:
            ao, back[h - 1] = lax.optimization_barrier((ao, back[h - 1]))
        back.append(backward(dhalo))
        outs.append(swap(ao) if last else exchange(ao[0].reshape(members, rows, -1)))
        mine.append(down)
    total = add(apart, *settle(mine, back[0]), back[1], members)
    outs[0], total = lax.optimization_barrier((outs[0], total))
    grad_k, grad_v = unpack(apart, swap(total, outs[-1], 5))
    attended, grad_q = spread(apart, *outs)
    return (attended, grad_q, grad_k, grad_v)


def solution(mesh):
    placed = P(("seq", "kvh"), None)
    return jax.shard_map(
        body, mesh=mesh, in_specs=(placed,) * 4, out_specs=(placed,) * 4, check_vma=False
    )
```

```python
import functools

import jax
import jax.numpy as jnp
from jax import lax
from jax.experimental import pallas as pl
from jax.experimental.pallas import tpu as pltpu
from jax.sharding import PartitionSpec as P

HEAD_DIM = 128
PAIR = 2 * HEAD_DIM
WINDOW = 1024
BLOCK = 128
CHUNKS = WINDOW // BLOCK + 1
SCORE_SCALE = 168.0 ** (-0.5)
EXP2_SCALE = SCORE_SCALE * 1.4426950408889634
EXCLUDED = -1e30
ONES = 16
IN_FLIGHT = 4
HOLD = 3
EARLY = 4

NN = (((1,), (0,)), ((), ()))
NT = (((1,), (1,)), ((), ()))

VMEM = pl.BlockSpec(memory_space=pltpu.VMEM)
ANY = pl.BlockSpec(memory_space=pl.ANY)
HBM = pl.BlockSpec(memory_space=pltpu.HBM)


def dot(left, right, dims):
    return lax.dot_general(left, right, dims, preferred_element_type=jnp.float32)


class Place:
    def __init__(self, apart):
        split = lax.axis_size("kvh")
        self.shard = lax.axis_index("seq")
        self.first = self.shard < apart
        self.member = lax.rem(self.shard, apart) * split + lax.axis_index("kvh")


def side_by_side(x):
    return jnp.concatenate([x[:, :HEAD_DIM].T, x[:, HEAD_DIM:].T], 1)


def attention_kernel(
    apart, taken, pieces, *refs
):
    place = Place(apart)
    qo_hbm, (halo_hbm, own_hbm, *refs) = refs[:taken], refs[taken:]
    ao_hbm, (dhalo_hbm, down_hbm, *refs) = refs[:pieces], refs[pieces:]
    (kv, qo, ao, dhalo, keys_t, values_t, acc_k, acc_v, exps0, exps1, scores0, scores1, tops, in_sem, q_sem, out_sem) = refs
    rows = qo.shape[0]
    blocks = rows // BLOCK
    whole = WINDOW // BLOCK
    exps, scores = (exps0, exps1), (scores0, scores1)

    def at(i):
        return pl.ds(pl.multiple_of(i * BLOCK, BLOCK), BLOCK)

    def span(i):
        return pl.ds(pl.multiple_of(i * BLOCK, BLOCK), CHUNKS * BLOCK)

    def qo_copy(i, piece=0):
        source = qo_hbm[0].at[at(i)] if taken == 1 else qo_hbm[piece]
        return pltpu.make_async_copy(source, qo.at[at(i)], q_sem.at[i])

    def ao_copy(i):
        return pltpu.make_async_copy(ao.at[at(i)], ao_hbm[0].at[at(i)], out_sem.at[0, i])

    def piece_copy(j):
        return pltpu.make_async_copy(ao.at[at(place.member ^ j)], ao_hbm[j], out_sem.at[0, j])

    def dhalo_copy(i):
        return pltpu.make_async_copy(dhalo.at[at(i)], dhalo_hbm.at[at(i)], out_sem.at[1, i])

    halo_copy = pltpu.make_async_copy(halo_hbm, kv.at[pl.ds(0, WINDOW)], in_sem.at[0])
    own_copy = pltpu.make_async_copy(own_hbm, kv.at[pl.ds(WINDOW, rows)], in_sem.at[1])
    halo_copy.start()
    own_copy.start()
    for i in range(blocks):
        (qo_copy(i) if taken == 1 else qo_copy(place.member ^ i, i)).start()

    ones_row = lax.broadcasted_iota(jnp.int32, (ONES, values_t.shape[1]), 0) == 0
    values_t[HEAD_DIM:, :] = jnp.where(ones_row, 1.0, 0.0).astype(jnp.bfloat16)
    acc_k[:, : WINDOW + BLOCK] = jnp.zeros((HEAD_DIM, WINDOW + BLOCK), jnp.float32)
    acc_v[:, : WINDOW + BLOCK] = jnp.zeros((HEAD_DIM, WINDOW + BLOCK), jnp.float32)
    key_at = lax.broadcasted_iota(jnp.int32, (BLOCK, 2 * BLOCK), 0)
    query_at = lax.broadcasted_iota(jnp.int32, (BLOCK, 2 * BLOCK), 1) & (BLOCK - 1)
    first = place.first

    def turn(c):
        keys_t[:, at(c)] = kv[at(c), :HEAD_DIM].T
        values_t[:HEAD_DIM, at(c)] = kv[at(c), HEAD_DIM:].T

    def bias(i, c):
        return jnp.where(first & (i + c < whole), EXCLUDED, 0.0).astype(jnp.float32)

    def score_dot(i):
        return dot(kv[span(i), :HEAD_DIM], side_by_side(qo[at(i), :PAIR]), NN)

    def keep_scores(slot, i, found):
        top = None
        for c in range(CHUNKS):
            part = found[c * BLOCK : (c + 1) * BLOCK]
            if c == 0:
                part = jnp.where(key_at > query_at, part, EXCLUDED)
            if c == CHUNKS - 1:
                part = jnp.where(key_at <= query_at, part, EXCLUDED)
            scores[slot][c * BLOCK : (c + 1) * BLOCK] = part
            high = jnp.max(part, axis=0, keepdims=True)
            if c < CHUNKS - 1:
                high = high + bias(i, c)
            top = high if top is None else jnp.maximum(top, high)
        tops[slot, :1] = top * EXP2_SCALE

    def exponentials(slot, i):
        top = tops[slot, :1]
        for c in range(CHUNKS):
            part = slice(c * BLOCK, (c + 1) * BLOCK)
            shift = top - bias(i, c) if c < CHUNKS - 1 else top
            exps[slot][part] = jnp.exp2(scores[slot][part] * EXP2_SCALE - shift).astype(jnp.bfloat16)

    def attended_of(slot, i, o_t):
        out = dot(values_t[:, span(i)], exps[slot][...], NN)
        inverse = 1.0 / out[HEAD_DIM : HEAD_DIM + 1]
        out = out[:HEAD_DIM] * inverse
        grad_out = o_t.astype(jnp.float32)
        delta = jnp.sum(out * grad_out, axis=0, keepdims=True)
        out = out.astype(jnp.bfloat16)
        ao[at(i), :HEAD_DIM] = out[:, :BLOCK].T
        ao[at(i), HEAD_DIM:PAIR] = out[:, BLOCK:].T
        return inverse, delta, (grad_out * inverse).astype(jnp.bfloat16)

    def score_gradients(slot, grad_weights, delta):
        grad_scores = []
        for c in range(CHUNKS):
            part = slice(c * BLOCK, (c + 1) * BLOCK)
            grad_scores.append(
                (exps[slot][part].astype(jnp.float32) * (grad_weights[part] - delta)).astype(jnp.bfloat16)
            )
        return jnp.concatenate(grad_scores, 0)

    def spend(i, grad_scores, inverse):
        q_t = side_by_side(qo[at(i), :PAIR])
        q_scaled = (q_t.astype(jnp.float32) * inverse).astype(jnp.bfloat16)
        grad_q = (dot(keys_t[:, span(i)], grad_scores, NN) * (inverse * SCORE_SCALE)).astype(jnp.bfloat16)
        ao[at(i), PAIR : PAIR + HEAD_DIM] = grad_q[:, :BLOCK].T
        ao[at(i), PAIR + HEAD_DIM :] = grad_q[:, BLOCK:].T
        acc_k[:, span(i)] += dot(q_scaled, grad_scores, NT)

    def flush(i):
        dhalo[at(i), :HEAD_DIM] = (acc_k[:, at(i)] * SCORE_SCALE).astype(jnp.bfloat16).T
        dhalo[at(i), HEAD_DIM:] = acc_v[:, at(i)].astype(jnp.bfloat16).T

    def stages(n, slot, begin=True, middle=True, end=True):
        if end:
            o_t = side_by_side(qo[at(n - 2), PAIR:])
            inverse, delta, o_scaled = attended_of(slot, n - 2, o_t)
            grad_weights = dot(kv[span(n - 2), HEAD_DIM:], o_t, NN)
        if begin:
            found = score_dot(n)
        if end:
            grad_scores = score_gradients(slot, grad_weights, delta)
            acc_v[:, span(n - 2)] += dot(o_scaled, exps[slot][...], NT)
        if middle:
            exponentials(1 - slot, n - 1)
        if begin:
            keep_scores(slot, n, found)
        if end:
            spend(n - 2, grad_scores, inverse)
            flush(n - 2)

    def extend(c):
        turn(c)
        acc_k[:, at(c)] = jnp.zeros((HEAD_DIM, BLOCK), jnp.float32)
        acc_v[:, at(c)] = jnp.zeros((HEAD_DIM, BLOCK), jnp.float32)

    def send(i):
        dhalo_copy(i).start()
        if pieces == 1:
            ao_copy(i).start()

    halo_copy.wait()
    own_copy.wait()
    qo_copy(0).wait()
    qo_copy(1).wait()
    stages(0, 0, middle=False, end=False)
    stages(1, 1, end=False)
    for c in range(whole + 1):
        turn(c)

    def step(j, carry):
        n = 2 * j
        qo_copy(n).wait()
        qo_copy(n + 1).wait()
        stages(n, 0)
        extend(n + whole - 1)
        stages(n + 1, 1)
        extend(n + whole)
        send(n - 2)
        send(n - 1)
        return carry

    lax.fori_loop(1, blocks // 2, step, 0)
    stages(blocks, 0, begin=False)
    extend(blocks + whole - 1)
    send(blocks - 2)
    stages(blocks + 1, 1, begin=False, middle=False)
    send(blocks - 1)
    if pieces > 1:
        for j in range(pieces):
            piece_copy(j).start()
    own_k = pltpu.make_async_copy(acc_k.at[:, pl.ds(WINDOW, rows)], down_hbm.at[0], in_sem.at[0])
    own_v = pltpu.make_async_copy(acc_v.at[:, pl.ds(WINDOW, rows)], down_hbm.at[1], in_sem.at[1])
    own_k.start()
    own_v.start()
    for i in range(blocks):
        (ao_copy(i) if pieces == 1 else piece_copy(i)).wait()
        dhalo_copy(i).wait()
    own_k.wait()
    own_v.wait()


def attention(apart, qo, halo, own, pieces):
    rows = own.shape[0]
    blocks = rows // BLOCK
    reach = WINDOW + rows
    bf16, f32 = jnp.bfloat16, jnp.float32
    width = 2 * PAIR
    return pl.pallas_call(
        functools.partial(attention_kernel, apart, len(qo), pieces),
        out_shape=(
            *[jax.ShapeDtypeStruct((rows // pieces, width), bf16)] * pieces,
            jax.ShapeDtypeStruct(halo.shape, bf16),
            jax.ShapeDtypeStruct((2, HEAD_DIM, rows), f32),
        ),
        in_specs=[ANY] * (len(qo) + 2),
        out_specs=(HBM,) * (pieces + 2),
        scratch_shapes=[
            pltpu.VMEM((reach, PAIR), bf16),
            pltpu.VMEM((rows, 2 * PAIR), bf16),
            pltpu.VMEM((rows, width), bf16),
            pltpu.VMEM(halo.shape, bf16),
            pltpu.VMEM((HEAD_DIM, reach + BLOCK), bf16),
            pltpu.VMEM((HEAD_DIM + ONES, reach + BLOCK), bf16),
            pltpu.VMEM((HEAD_DIM, reach + BLOCK), f32),
            pltpu.VMEM((HEAD_DIM, reach + BLOCK), f32),
            pltpu.VMEM((CHUNKS * BLOCK, 2 * BLOCK), bf16),
            pltpu.VMEM((CHUNKS * BLOCK, 2 * BLOCK), bf16),
            pltpu.VMEM((CHUNKS * BLOCK, 2 * BLOCK), f32),
            pltpu.VMEM((CHUNKS * BLOCK, 2 * BLOCK), f32),
            pltpu.VMEM((2, 8, 2 * BLOCK), f32),
            pltpu.SemaphoreType.DMA((2,)),
            pltpu.SemaphoreType.DMA((blocks,)),
            pltpu.SemaphoreType.DMA((2, blocks)),
        ],
        compiler_params=pltpu.CompilerParams(vmem_limit_bytes=58 * 2**20),
        cost_estimate=pl.CostEstimate(flops=10**10, bytes_accessed=4 * 2**20, transcendentals=0),
        name="attention",
    )(*qo, halo, own)


def interleave_kernel(apart, width, sets, *refs):
    place = Place(apart)
    arrays, refs = refs[:2], refs[2:]
    groups = arrays[0].shape[1] // sets[0][1][0][2]
    outs, refs = refs[: -(4 + len(sets))], refs[-(4 + len(sets)) :]
    fetched, staged, (in_sem, out_sem) = refs[:2], refs[2:-2], refs[-2:]
    loads = [pltpu.make_async_copy(arrays[n], fetched[n], in_sem.at[n]) for n in range(2)]
    for load in loads:
        load.start()
    for load in loads:
        load.wait()
    stores = []
    taken = 0
    for k, (split, parts) in enumerate(sets):
        for g in range(groups):
            source = place.member ^ g if split else g
            for n, (which, start, stride) in enumerate(parts):
                at = source * stride + start
                if split:
                    at = pl.multiple_of(at, HEAD_DIM)
                staged[k][g, :, n * width : (n + 1) * width] = fetched[which][:, pl.ds(at, width)]
            out = outs[taken + g] if split else outs[taken].at[g]
            stores.append(pltpu.make_async_copy(staged[k].at[g], out, out_sem.at[k, g]))
            stores[-1].start()
        taken += groups if split else 1
    for store in stores:
        store.wait()


def interleave(apart, arrays, groups, width, sets):
    rows, cols = arrays[0].shape
    dtype = arrays[0].dtype
    shapes, staged = [], []
    for split, parts in sets:
        whole = (groups, rows, width * len(parts))
        staged.append(pltpu.VMEM(whole, dtype))
        shapes += [jax.ShapeDtypeStruct(whole[1:], dtype)] * groups if split else [jax.ShapeDtypeStruct(whole, dtype)]
    return pl.pallas_call(
        functools.partial(interleave_kernel, apart, width, sets),
        out_shape=tuple(shapes),
        in_specs=[HBM, HBM],
        out_specs=(HBM,) * len(shapes),
        scratch_shapes=[
            pltpu.VMEM((rows, cols), dtype),
            pltpu.VMEM((rows, cols), dtype),
            *staged,
            pltpu.SemaphoreType.DMA((2,)),
            pltpu.SemaphoreType.DMA((len(sets), groups)),
        ],
        compiler_params=pltpu.CompilerParams(vmem_limit_bytes=58 * 2**20),
        name="interleave",
    )(*arrays)


def assemble_kernel(apart, *refs):
    place = Place(apart)
    *arrays, sem = refs
    count, heads = sem.shape
    pieces, outs = arrays[:count], arrays[count:]
    rows, width = pieces[0].shape[0], outs[0].shape[1]
    copies = []
    for j in range(count):
        at = pl.ds(pl.multiple_of((place.member ^ j) * rows, BLOCK), rows)
        for h in range(heads):
            source = pieces[j].at[:, pl.ds(h * width, width)]
            copies.append(pltpu.make_async_copy(source, outs[h].at[at], sem.at[j, h]))
    for copy in copies:
        copy.start()
    for copy in copies:
        copy.wait()


def assemble(apart, pieces, heads):
    rows, width = pieces[0].shape
    shape = jax.ShapeDtypeStruct((len(pieces) * rows, width // heads), pieces[0].dtype)
    return pl.pallas_call(
        functools.partial(assemble_kernel, apart),
        out_shape=(shape,) * heads,
        in_specs=[ANY] * len(pieces),
        out_specs=(VMEM,) * heads,
        scratch_shapes=[pltpu.SemaphoreType.DMA((len(pieces), heads))],
        compiler_params=pltpu.CompilerParams(vmem_limit_bytes=8 * 2**20),
        name="assemble",
    )(*pieces)


def group_at(place, j, width):
    return pl.multiple_of((place.member ^ j) * width, HEAD_DIM)


def spread_kernel(apart, x_ref, *refs):
    place = Place(apart)
    *pieces, a_ref, b_ref = refs
    groups, _, width = x_ref.shape
    half = width // 2
    for g in range(groups):
        a_ref[:, g * width : g * width + half] = x_ref[g, :, :half]
        b_ref[:, g * width : g * width + half] = x_ref[g, :, half:]
        cols = pl.ds(group_at(place, g, width) + half, half)
        a_ref[:, cols] = pieces[g][:, :half]
        b_ref[:, cols] = pieces[g][:, half:]


def spread(apart, x, pieces):
    groups, rows, width = x.shape
    shape = jax.ShapeDtypeStruct((rows, groups * width), x.dtype)
    return pl.pallas_call(
        functools.partial(spread_kernel, apart),
        out_shape=(shape, shape),
        in_specs=[VMEM] * (groups + 1),
        out_specs=(VMEM, VMEM),
        compiler_params=pltpu.CompilerParams(vmem_limit_bytes=16 * 2**20),
        name="spread",
    )(x, *pieces)


def settle_kernel(own0, own1, back0, done_ref, open_ref):
    for n, scale in enumerate((SCORE_SCALE, 1.0)):
        cols = slice(n * HEAD_DIM, (n + 1) * HEAD_DIM)
        for i in range(done_ref.shape[0] // BLOCK):
            at = slice(i * BLOCK, (i + 1) * BLOCK)
            total = (own0[n, :, at] * scale).T + back0[at, cols].astype(jnp.float32)
            done_ref[at, cols] = total.astype(jnp.bfloat16)
            open_ref[at, cols] = (own1[n, :, at] * scale).T


def settle(own, back):
    return pl.pallas_call(
        settle_kernel,
        out_shape=(
            jax.ShapeDtypeStruct(back.shape, jnp.bfloat16),
            jax.ShapeDtypeStruct(back.shape, jnp.float32),
        ),
        in_specs=[VMEM] * 3,
        out_specs=(VMEM,) * 2,
        compiler_params=pltpu.CompilerParams(vmem_limit_bytes=16 * 2**20),
        name="settle",
    )(*own, back)


def add_kernel(apart, done_ref, open_ref, back_ref, *out_refs):
    place = Place(apart)
    rows = out_refs[0].shape[0]
    for j, out_ref in enumerate(out_refs):
        at = pl.ds(group_at(place, j, rows), rows)
        out_ref[:, :PAIR] = done_ref[at, :]
        out_ref[:, PAIR:] = (open_ref[at, :] + back_ref[at, :].astype(jnp.float32)).astype(jnp.bfloat16)


def add(apart, done, started, back, groups):
    rows, width = back.shape
    shape = jax.ShapeDtypeStruct((rows // groups, 2 * width), jnp.bfloat16)
    return pl.pallas_call(
        functools.partial(add_kernel, apart),
        out_shape=(shape,) * groups,
        in_specs=[VMEM] * 3,
        out_specs=(VMEM,) * groups,
        compiler_params=pltpu.CompilerParams(vmem_limit_bytes=16 * 2**20),
        name="add",
    )(done, started, back)


def unpack_kernel(apart, *refs):
    place = Place(apart)
    *pieces, a_ref, b_ref = refs
    heads = pieces[0].shape[1] // PAIR
    for j, piece in enumerate(pieces):
        start = group_at(place, j, heads * HEAD_DIM)
        for h in range(heads):
            cols = pl.ds(start + h * HEAD_DIM, HEAD_DIM)
            a_ref[:, cols] = piece[:, h * PAIR : h * PAIR + HEAD_DIM]
            b_ref[:, cols] = piece[:, h * PAIR + HEAD_DIM : (h + 1) * PAIR]


def unpack(apart, pieces):
    rows, width = pieces[0].shape
    shape = jax.ShapeDtypeStruct((rows, len(pieces) * width // 2), pieces[0].dtype)
    return pl.pallas_call(
        functools.partial(unpack_kernel, apart),
        out_shape=(shape, shape),
        in_specs=[VMEM] * len(pieces),
        out_specs=(VMEM, VMEM),
        compiler_params=pltpu.CompilerParams(vmem_limit_bytes=16 * 2**20),
        name="unpack",
    )(*pieces)


def body(queries, key_rows, value_rows, grad_out):
    shards, split = lax.axis_size("seq"), lax.axis_size("kvh")
    rows = queries.shape[0]
    apart = WINDOW // (rows * split)
    members = apart * split
    heads = key_rows.shape[1] // (members * HEAD_DIM)
    groups = [[g * members + i for i in range(members)] for g in range(shards // apart)]
    def exchange(x):
        return lax.all_to_all(x, ("seq", "kvh"), 0, 0, tiled=True, axis_index_groups=groups)

    order = sorted(range(1, members), key=lambda j: j == 1)

    def swap(pieces, before=None, limit=IN_FLIGHT):
        every = range(shards * split)
        out = [pieces[0]] * members
        sent = [] if before is None else [(before, j) for j in order]
        for j in order:
            piece = pieces[j]
            if len(sent) >= limit:
                box, k = sent[-limit]
                piece, box[k] = lax.optimization_barrier((piece, box[k]))
            out[j] = lax.ppermute(piece, ("seq", "kvh"), [(i, i ^ j) for i in every])
            sent.append((out, j))
        return out

    def onward(x):
        return lax.ppermute(x, "seq", [(i, (i + apart) % shards) for i in range(shards)])

    def backward(x):
        return lax.ppermute(x, "seq", [((i + apart) % shards, i) for i in range(shards)])

    stride = heads * HEAD_DIM
    kv_parts = [(n, h * HEAD_DIM, stride) for h in range(heads) for n in range(2)]
    def qo_parts(h):
        return [(n, h * PAIR, 2 * stride) for n in range(2)]

    kv = list(interleave(apart, (key_rows, value_rows), members, HEAD_DIM, [(True, kv_parts)]))
    sets = [(h == 0, qo_parts(h)) for h in range(heads)]
    packed = interleave(apart, (queries, grad_out), members, PAIR, sets)
    late = order[EARLY]
    kv[late], (*first, second) = lax.optimization_barrier((kv[late], packed))
    kv = swap(kv, None, 5)
    first = swap(first, kv, 5)
    own = assemble(apart, kv, heads)
    second, first[order[HOLD]] = lax.optimization_barrier((second, first[order[HOLD]]))
    qos = [first, [exchange(second).reshape(WINDOW, -1)]]
    held, first[order[-2]] = lax.optimization_barrier((own[1], first[order[-2]]))
    halos = [onward(own[0]), onward(held)]
    outs, mine, back = [], [], []
    for h in range(heads):
        last = h == heads - 1
        *ao, dhalo, down = attention(apart, qos[h], halos[h], own[h], members if last else 1)
        if last:
            ao, back[h - 1] = lax.optimization_barrier((ao, back[h - 1]))
        back.append(backward(dhalo))
        outs.append(swap(ao) if last else exchange(ao[0].reshape(members, rows, -1)))
        mine.append(down)
    total = add(apart, *settle(mine, back[0]), back[1], members)
    outs[0], total = lax.optimization_barrier((outs[0], total))
    grad_k, grad_v = unpack(apart, swap(total, outs[-1], 5))
    attended, grad_q = spread(apart, *outs)
    return (attended, grad_q, grad_k, grad_v)


def solution(mesh):
    placed = P(("seq", "kvh"), None)
    return jax.shard_map(
        body, mesh=mesh, in_specs=(placed,) * 4, out_specs=(placed,) * 4, check_vma=False
    )
```

```python
import functools

import jax
import jax.numpy as jnp
from jax import lax
from jax.experimental import pallas as pl
from jax.experimental.pallas import tpu as pltpu
from jax.sharding import PartitionSpec as P

HEAD_DIM = 128
PAIR = 2 * HEAD_DIM
WINDOW = 1024
BLOCK = 128
CHUNKS = WINDOW // BLOCK + 1
SCORE_SCALE = 168.0 ** (-0.5)
EXP2_SCALE = SCORE_SCALE * 1.4426950408889634
EXCLUDED = -1e30
ONES = 16
IN_FLIGHT = 4
HOLD = 3
WAITS = 5
EARLY = 4

NN = (((1,), (0,)), ((), ()))
NT = (((1,), (1,)), ((), ()))

VMEM = pl.BlockSpec(memory_space=pltpu.VMEM)
ANY = pl.BlockSpec(memory_space=pl.ANY)
HBM = pl.BlockSpec(memory_space=pltpu.HBM)


def dot(left, right, dims):
    return lax.dot_general(left, right, dims, preferred_element_type=jnp.float32)


class Place:
    def __init__(self, apart):
        split = lax.axis_size("kvh")
        self.shard = lax.axis_index("seq")
        self.first = self.shard < apart
        self.member = lax.rem(self.shard, apart) * split + lax.axis_index("kvh")


def side_by_side(x):
    return jnp.concatenate([x[:, :HEAD_DIM].T, x[:, HEAD_DIM:].T], 1)


def attention_kernel(
    apart, taken, pieces, *refs
):
    place = Place(apart)
    qo_hbm, (halo_hbm, own_hbm, *refs) = refs[:taken], refs[taken:]
    ao_hbm, (dhalo_hbm, down_hbm, *refs) = refs[:pieces], refs[pieces:]
    (kv, qo, ao, dhalo, keys_t, values_t, acc_k, acc_v, exps0, exps1, scores0, scores1, tops, in_sem, q_sem, out_sem) = refs
    rows = qo.shape[0]
    blocks = rows // BLOCK
    whole = WINDOW // BLOCK
    exps, scores = (exps0, exps1), (scores0, scores1)

    def at(i):
        return pl.ds(pl.multiple_of(i * BLOCK, BLOCK), BLOCK)

    def chunks_of(i, near):
        return i + 1 if near else CHUNKS

    def span(i, near):
        start = WINDOW if near else pl.multiple_of(i * BLOCK, BLOCK)
        return pl.ds(start, chunks_of(i, near) * BLOCK)

    def qo_copy(i, piece=0):
        source = qo_hbm[0].at[at(i)] if taken == 1 else qo_hbm[piece]
        return pltpu.make_async_copy(source, qo.at[at(i)], q_sem.at[i])

    def ao_copy(i):
        return pltpu.make_async_copy(ao.at[at(i)], ao_hbm[0].at[at(i)], out_sem.at[0, i])

    def piece_copy(j):
        return pltpu.make_async_copy(ao.at[at(place.member ^ j)], ao_hbm[j], out_sem.at[0, j])

    def dhalo_copy(i):
        return pltpu.make_async_copy(dhalo.at[at(i)], dhalo_hbm.at[at(i)], out_sem.at[1, i])

    halo_copy = pltpu.make_async_copy(halo_hbm, kv.at[pl.ds(0, WINDOW)], in_sem.at[0])
    own_copy = pltpu.make_async_copy(own_hbm, kv.at[pl.ds(WINDOW, rows)], in_sem.at[1])
    halo_copy.start()
    own_copy.start()
    for i in range(blocks):
        (qo_copy(i) if taken == 1 else qo_copy(place.member ^ i, i)).start()

    ones_row = lax.broadcasted_iota(jnp.int32, (ONES, values_t.shape[1]), 0) == 0
    values_t[HEAD_DIM:, :] = jnp.where(ones_row, 1.0, 0.0).astype(jnp.bfloat16)
    acc_k[:, : WINDOW + BLOCK] = jnp.zeros((HEAD_DIM, WINDOW + BLOCK), jnp.float32)
    acc_v[:, : WINDOW + BLOCK] = jnp.zeros((HEAD_DIM, WINDOW + BLOCK), jnp.float32)
    key_at = lax.broadcasted_iota(jnp.int32, (BLOCK, 2 * BLOCK), 0)
    query_at = lax.broadcasted_iota(jnp.int32, (BLOCK, 2 * BLOCK), 1) & (BLOCK - 1)
    def turn(c):
        keys_t[:, at(c)] = kv[at(c), :HEAD_DIM].T
        values_t[:HEAD_DIM, at(c)] = kv[at(c), HEAD_DIM:].T

    def score_dot(i, near):
        return dot(kv[span(i, near), :HEAD_DIM], side_by_side(qo[at(i), :PAIR]), NN)

    def keep_scores(slot, i, found, near):
        top = None
        count = chunks_of(i, near)
        for c in range(count):
            part = found[c * BLOCK : (c + 1) * BLOCK]
            if c == 0 and not near:
                part = jnp.where(key_at > query_at, part, EXCLUDED)
            if c == count - 1:
                part = jnp.where(key_at <= query_at, part, EXCLUDED)
            scores[slot][c * BLOCK : (c + 1) * BLOCK] = part
            high = jnp.max(part, axis=0, keepdims=True)
            top = high if top is None else jnp.maximum(top, high)
        tops[slot, :1] = top * EXP2_SCALE

    def exponentials(slot, i, near):
        top = tops[slot, :1]
        for c in range(chunks_of(i, near)):
            part = slice(c * BLOCK, (c + 1) * BLOCK)
            exps[slot][part] = jnp.exp2(scores[slot][part] * EXP2_SCALE - top).astype(jnp.bfloat16)

    def attended_of(slot, i, o_t, low, near):
        out = dot(values_t[:, span(i, near)], low, NN)
        inverse = 1.0 / out[HEAD_DIM : HEAD_DIM + 1]
        out = out[:HEAD_DIM] * inverse
        grad_out = o_t.astype(jnp.float32)
        delta = jnp.sum(out * grad_out, axis=0, keepdims=True)
        out = out.astype(jnp.bfloat16)
        ao[at(i), :HEAD_DIM] = out[:, :BLOCK].T
        ao[at(i), HEAD_DIM:PAIR] = out[:, BLOCK:].T
        return inverse, delta, (grad_out * inverse).astype(jnp.bfloat16)

    def score_gradients(slot, i, grad_weights, delta, near):
        grad_scores = []
        for c in range(chunks_of(i, near)):
            part = slice(c * BLOCK, (c + 1) * BLOCK)
            grad_scores.append(
                (exps[slot][part].astype(jnp.float32) * (grad_weights[part] - delta)).astype(jnp.bfloat16)
            )
        return jnp.concatenate(grad_scores, 0)

    def spend(i, grad_scores, inverse, near):
        q_t = side_by_side(qo[at(i), :PAIR])
        q_scaled = (q_t.astype(jnp.float32) * inverse).astype(jnp.bfloat16)
        grad_q = (dot(keys_t[:, span(i, near)], grad_scores, NN) * (inverse * SCORE_SCALE)).astype(jnp.bfloat16)
        ao[at(i), PAIR : PAIR + HEAD_DIM] = grad_q[:, :BLOCK].T
        ao[at(i), PAIR + HEAD_DIM :] = grad_q[:, BLOCK:].T
        acc_k[:, span(i, near)] += dot(q_scaled, grad_scores, NT)

    def flush(i):
        dhalo[at(i), :HEAD_DIM] = (acc_k[:, at(i)] * SCORE_SCALE).astype(jnp.bfloat16).T
        dhalo[at(i), HEAD_DIM:] = acc_v[:, at(i)].astype(jnp.bfloat16).T

    def stages(n, slot, begin=True, middle=True, end=True, near=False):
        if end:
            o_t = side_by_side(qo[at(n - 2), PAIR:])
            low = exps[slot][: chunks_of(n - 2, near) * BLOCK]
            inverse, delta, o_scaled = attended_of(slot, n - 2, o_t, low, near)
            grad_weights = dot(kv[span(n - 2, near), HEAD_DIM:], o_t, NN)
        if begin:
            found = score_dot(n, near)
        if end:
            grad_scores = score_gradients(slot, n - 2, grad_weights, delta, near)
            acc_v[:, span(n - 2, near)] += dot(o_scaled, low, NT)
        if middle:
            exponentials(1 - slot, n - 1, near)
        if begin:
            keep_scores(slot, n, found, near)
        if end:
            spend(n - 2, grad_scores, inverse, near)
            if not near:
                flush(n - 2)

    def extend(c):
        turn(c)
        acc_k[:, at(c)] = jnp.zeros((HEAD_DIM, BLOCK), jnp.float32)
        acc_v[:, at(c)] = jnp.zeros((HEAD_DIM, BLOCK), jnp.float32)

    def send(i):
        dhalo_copy(i).start()
        if pieces == 1:
            ao_copy(i).start()

    halo_copy.wait()
    own_copy.wait()
    qo_copy(0).wait()
    qo_copy(1).wait()

    @pl.when(jnp.logical_not(place.first))
    def _():
        stages(0, 0, middle=False, end=False)
        stages(1, 1, end=False)
        for c in range(whole + 1):
            turn(c)

        def step(j, carry):
            n = 2 * j
            qo_copy(n).wait()
            qo_copy(n + 1).wait()
            stages(n, 0)
            extend(n + whole - 1)
            stages(n + 1, 1)
            extend(n + whole)
            send(n - 2)
            send(n - 1)
            return carry

        lax.fori_loop(1, blocks // 2, step, 0)
        stages(blocks, 0, begin=False)
        extend(blocks + whole - 1)
        send(blocks - 2)
        stages(blocks + 1, 1, begin=False, middle=False)
        send(blocks - 1)

    @pl.when(place.first)
    def _():
        dhalo[...] = jnp.zeros_like(dhalo)
        for n in range(blocks + 2):
            if 2 <= n < blocks:
                qo_copy(n).wait()
            if n >= 2:
                extend(whole + n - 2)
            stages(n, n % 2, n < blocks, 1 <= n <= blocks, n >= 2, near=True)
            if n >= 2:
                send(n - 2)

    if pieces > 1:
        for j in range(pieces):
            piece_copy(j).start()
    own_k = pltpu.make_async_copy(acc_k.at[:, pl.ds(WINDOW, rows)], down_hbm.at[0], in_sem.at[0])
    own_v = pltpu.make_async_copy(acc_v.at[:, pl.ds(WINDOW, rows)], down_hbm.at[1], in_sem.at[1])
    own_k.start()
    own_v.start()
    for i in range(blocks):
        (ao_copy(i) if pieces == 1 else piece_copy(i)).wait()
        dhalo_copy(i).wait()
    own_k.wait()
    own_v.wait()


def attention(apart, qo, halo, own, pieces):
    rows = own.shape[0]
    blocks = rows // BLOCK
    reach = WINDOW + rows
    bf16, f32 = jnp.bfloat16, jnp.float32
    width = 2 * PAIR
    return pl.pallas_call(
        functools.partial(attention_kernel, apart, len(qo), pieces),
        out_shape=(
            *[jax.ShapeDtypeStruct((rows // pieces, width), bf16)] * pieces,
            jax.ShapeDtypeStruct(halo.shape, bf16),
            jax.ShapeDtypeStruct((2, HEAD_DIM, rows), f32),
        ),
        in_specs=[ANY] * (len(qo) + 2),
        out_specs=(HBM,) * (pieces + 2),
        scratch_shapes=[
            pltpu.VMEM((reach, PAIR), bf16),
            pltpu.VMEM((rows, 2 * PAIR), bf16),
            pltpu.VMEM((rows, width), bf16),
            pltpu.VMEM(halo.shape, bf16),
            pltpu.VMEM((HEAD_DIM, reach + BLOCK), bf16),
            pltpu.VMEM((HEAD_DIM + ONES, reach + BLOCK), bf16),
            pltpu.VMEM((HEAD_DIM, reach + BLOCK), f32),
            pltpu.VMEM((HEAD_DIM, reach + BLOCK), f32),
            pltpu.VMEM((CHUNKS * BLOCK, 2 * BLOCK), bf16),
            pltpu.VMEM((CHUNKS * BLOCK, 2 * BLOCK), bf16),
            pltpu.VMEM((CHUNKS * BLOCK, 2 * BLOCK), f32),
            pltpu.VMEM((CHUNKS * BLOCK, 2 * BLOCK), f32),
            pltpu.VMEM((2, 8, 2 * BLOCK), f32),
            pltpu.SemaphoreType.DMA((2,)),
            pltpu.SemaphoreType.DMA((blocks,)),
            pltpu.SemaphoreType.DMA((2, blocks)),
        ],
        compiler_params=pltpu.CompilerParams(vmem_limit_bytes=58 * 2**20),
        cost_estimate=pl.CostEstimate(flops=10**10, bytes_accessed=4 * 2**20, transcendentals=0),
        name="attention",
    )(*qo, halo, own)


def interleave_kernel(apart, width, sets, *refs):
    place = Place(apart)
    arrays, refs = refs[:2], refs[2:]
    groups = arrays[0].shape[1] // sets[0][1][0][2]
    outs, refs = refs[: -(4 + len(sets))], refs[-(4 + len(sets)) :]
    fetched, staged, (in_sem, out_sem) = refs[:2], refs[2:-2], refs[-2:]
    loads = [pltpu.make_async_copy(arrays[n], fetched[n], in_sem.at[n]) for n in range(2)]
    for load in loads:
        load.start()
    for load in loads:
        load.wait()
    stores = []
    taken = 0
    for k, (split, parts) in enumerate(sets):
        for g in range(groups):
            source = place.member ^ g if split else g
            for n, (which, start, stride) in enumerate(parts):
                at = source * stride + start
                if split:
                    at = pl.multiple_of(at, HEAD_DIM)
                staged[k][g, :, n * width : (n + 1) * width] = fetched[which][:, pl.ds(at, width)]
            out = outs[taken + g] if split else outs[taken].at[g]
            stores.append(pltpu.make_async_copy(staged[k].at[g], out, out_sem.at[k, g]))
            stores[-1].start()
        taken += groups if split else 1
    for store in stores:
        store.wait()


def interleave(apart, arrays, groups, width, sets):
    rows, cols = arrays[0].shape
    dtype = arrays[0].dtype
    shapes, staged = [], []
    for split, parts in sets:
        whole = (groups, rows, width * len(parts))
        staged.append(pltpu.VMEM(whole, dtype))
        shapes += [jax.ShapeDtypeStruct(whole[1:], dtype)] * groups if split else [jax.ShapeDtypeStruct(whole, dtype)]
    return pl.pallas_call(
        functools.partial(interleave_kernel, apart, width, sets),
        out_shape=tuple(shapes),
        in_specs=[HBM, HBM],
        out_specs=(HBM,) * len(shapes),
        scratch_shapes=[
            pltpu.VMEM((rows, cols), dtype),
            pltpu.VMEM((rows, cols), dtype),
            *staged,
            pltpu.SemaphoreType.DMA((2,)),
            pltpu.SemaphoreType.DMA((len(sets), groups)),
        ],
        compiler_params=pltpu.CompilerParams(vmem_limit_bytes=58 * 2**20),
        name="interleave",
    )(*arrays)


def assemble_kernel(apart, *refs):
    place = Place(apart)
    *arrays, sem = refs
    count, heads = sem.shape
    pieces, outs = arrays[:count], arrays[count:]
    rows, width = pieces[0].shape[0], outs[0].shape[1]
    copies = []
    for j in range(count):
        at = pl.ds(pl.multiple_of((place.member ^ j) * rows, BLOCK), rows)
        for h in range(heads):
            source = pieces[j].at[:, pl.ds(h * width, width)]
            copies.append(pltpu.make_async_copy(source, outs[h].at[at], sem.at[j, h]))
    for copy in copies:
        copy.start()
    for copy in copies:
        copy.wait()


def assemble(apart, pieces, heads):
    rows, width = pieces[0].shape
    shape = jax.ShapeDtypeStruct((len(pieces) * rows, width // heads), pieces[0].dtype)
    return pl.pallas_call(
        functools.partial(assemble_kernel, apart),
        out_shape=(shape,) * heads,
        in_specs=[ANY] * len(pieces),
        out_specs=(VMEM,) * heads,
        scratch_shapes=[pltpu.SemaphoreType.DMA((len(pieces), heads))],
        compiler_params=pltpu.CompilerParams(vmem_limit_bytes=8 * 2**20),
        name="assemble",
    )(*pieces)


def group_at(place, j, width):
    return pl.multiple_of((place.member ^ j) * width, HEAD_DIM)


def spread_kernel(apart, x_ref, *refs):
    place = Place(apart)
    *pieces, a_ref, b_ref = refs
    groups, _, width = x_ref.shape
    half = width // 2
    for g in range(groups):
        a_ref[:, g * width : g * width + half] = x_ref[g, :, :half]
        b_ref[:, g * width : g * width + half] = x_ref[g, :, half:]
        cols = pl.ds(group_at(place, g, width) + half, half)
        a_ref[:, cols] = pieces[g][:, :half]
        b_ref[:, cols] = pieces[g][:, half:]


def spread(apart, x, pieces):
    groups, rows, width = x.shape
    shape = jax.ShapeDtypeStruct((rows, groups * width), x.dtype)
    return pl.pallas_call(
        functools.partial(spread_kernel, apart),
        out_shape=(shape, shape),
        in_specs=[VMEM] * (groups + 1),
        out_specs=(VMEM, VMEM),
        compiler_params=pltpu.CompilerParams(vmem_limit_bytes=16 * 2**20),
        name="spread",
    )(x, *pieces)


def settle_kernel(own0, own1, back0, done_ref, open_ref):
    for n, scale in enumerate((SCORE_SCALE, 1.0)):
        cols = slice(n * HEAD_DIM, (n + 1) * HEAD_DIM)
        for i in range(done_ref.shape[0] // BLOCK):
            at = slice(i * BLOCK, (i + 1) * BLOCK)
            total = (own0[n, :, at] * scale).T + back0[at, cols].astype(jnp.float32)
            done_ref[at, cols] = total.astype(jnp.bfloat16)
            open_ref[at, cols] = (own1[n, :, at] * scale).T


def settle(own, back):
    return pl.pallas_call(
        settle_kernel,
        out_shape=(
            jax.ShapeDtypeStruct(back.shape, jnp.bfloat16),
            jax.ShapeDtypeStruct(back.shape, jnp.float32),
        ),
        in_specs=[VMEM] * 3,
        out_specs=(VMEM,) * 2,
        compiler_params=pltpu.CompilerParams(vmem_limit_bytes=16 * 2**20),
        name="settle",
    )(*own, back)


def add_kernel(apart, done_ref, open_ref, back_ref, *out_refs):
    place = Place(apart)
    rows = out_refs[0].shape[0]
    for j, out_ref in enumerate(out_refs):
        at = pl.ds(group_at(place, j, rows), rows)
        out_ref[:, :PAIR] = done_ref[at, :]
        out_ref[:, PAIR:] = (open_ref[at, :] + back_ref[at, :].astype(jnp.float32)).astype(jnp.bfloat16)


def add(apart, done, started, back, groups):
    rows, width = back.shape
    shape = jax.ShapeDtypeStruct((rows // groups, 2 * width), jnp.bfloat16)
    return pl.pallas_call(
        functools.partial(add_kernel, apart),
        out_shape=(shape,) * groups,
        in_specs=[VMEM] * 3,
        out_specs=(VMEM,) * groups,
        compiler_params=pltpu.CompilerParams(vmem_limit_bytes=16 * 2**20),
        name="add",
    )(done, started, back)


def unpack_kernel(apart, *refs):
    place = Place(apart)
    *pieces, a_ref, b_ref = refs
    heads = pieces[0].shape[1] // PAIR
    for j, piece in enumerate(pieces):
        start = group_at(place, j, heads * HEAD_DIM)
        for h in range(heads):
            cols = pl.ds(start + h * HEAD_DIM, HEAD_DIM)
            a_ref[:, cols] = piece[:, h * PAIR : h * PAIR + HEAD_DIM]
            b_ref[:, cols] = piece[:, h * PAIR + HEAD_DIM : (h + 1) * PAIR]


def unpack(apart, pieces):
    rows, width = pieces[0].shape
    shape = jax.ShapeDtypeStruct((rows, len(pieces) * width // 2), pieces[0].dtype)
    return pl.pallas_call(
        functools.partial(unpack_kernel, apart),
        out_shape=(shape, shape),
        in_specs=[VMEM] * len(pieces),
        out_specs=(VMEM, VMEM),
        compiler_params=pltpu.CompilerParams(vmem_limit_bytes=16 * 2**20),
        name="unpack",
    )(*pieces)


def body(queries, key_rows, value_rows, grad_out):
    shards, split = lax.axis_size("seq"), lax.axis_size("kvh")
    rows = queries.shape[0]
    apart = WINDOW // (rows * split)
    members = apart * split
    heads = key_rows.shape[1] // (members * HEAD_DIM)
    groups = [[g * members + i for i in range(members)] for g in range(shards // apart)]
    def exchange(x):
        return lax.all_to_all(x, ("seq", "kvh"), 0, 0, tiled=True, axis_index_groups=groups)

    order = sorted(range(1, members), key=lambda j: j == 1)

    def swap(pieces, before=None, limit=IN_FLIGHT):
        every = range(shards * split)
        out = [pieces[0]] * members
        sent = [] if before is None else [(before, j) for j in order]
        for j in order:
            piece = pieces[j]
            if len(sent) >= limit:
                box, k = sent[-limit]
                piece, box[k] = lax.optimization_barrier((piece, box[k]))
            out[j] = lax.ppermute(piece, ("seq", "kvh"), [(i, i ^ j) for i in every])
            sent.append((out, j))
        return out

    def onward(x):
        return lax.ppermute(x, "seq", [(i, (i + apart) % shards) for i in range(shards)])

    def backward(x):
        return lax.ppermute(x, "seq", [((i + apart) % shards, i) for i in range(shards)])

    stride = heads * HEAD_DIM
    kv_parts = [(n, h * HEAD_DIM, stride) for h in range(heads) for n in range(2)]
    def qo_parts(h):
        return [(n, h * PAIR, 2 * stride) for n in range(2)]

    kv = list(interleave(apart, (key_rows, value_rows), members, HEAD_DIM, [(True, kv_parts)]))
    sets = [(h == 0, qo_parts(h)) for h in range(heads)]
    packed = interleave(apart, (queries, grad_out), members, PAIR, sets)
    late = order[EARLY]
    kv[late], (*first, second) = lax.optimization_barrier((kv[late], packed))
    kv = swap(kv, None, 5)
    first = swap(first, kv, 5)
    own = assemble(apart, kv, heads)
    second, first[order[HOLD]] = lax.optimization_barrier((second, first[order[HOLD]]))
    qos = [first, [exchange(second).reshape(WINDOW, -1)]]
    held, first[order[-2]] = lax.optimization_barrier((own[1], first[order[-2]]))
    halos = [onward(own[0]), onward(held)]
    outs, mine, back = [], [], []
    for h in range(heads):
        last = h == heads - 1
        *ao, dhalo, down = attention(apart, qos[h], halos[h], own[h], members if last else 1)
        if last:
            ao[order[WAITS]], back[h - 1] = lax.optimization_barrier((ao[order[WAITS]], back[h - 1]))
        back.append(backward(dhalo))
        outs.append(swap(ao) if last else exchange(ao[0].reshape(members, rows, -1)))
        mine.append(down)
    total = add(apart, *settle(mine, back[0]), back[1], members)
    outs[0], total = lax.optimization_barrier((outs[0], total))
    grad_k, grad_v = unpack(apart, swap(total, outs[-1], 5))
    attended, grad_q = spread(apart, *outs)
    return (attended, grad_q, grad_k, grad_v)


def solution(mesh):
    placed = P(("seq", "kvh"), None)
    return jax.shard_map(
        body, mesh=mesh, in_specs=(placed,) * 4, out_specs=(placed,) * 4, check_vma=False
    )
```

```python
import functools

import jax
import jax.numpy as jnp
from jax import lax
from jax.experimental import pallas as pl
from jax.experimental.pallas import tpu as pltpu
from jax.sharding import PartitionSpec as P

HEAD_DIM = 128
PAIR = 2 * HEAD_DIM
WINDOW = 1024
BLOCK = 128
CHUNKS = WINDOW // BLOCK + 1
SCORE_SCALE = 168.0 ** (-0.5)
EXP2_SCALE = SCORE_SCALE * 1.4426950408889634
EXCLUDED = -1e30
ONES = 16
IN_FLIGHT = 4
HOLD = 3
WAITS = 5
EARLY = 4

NN = (((1,), (0,)), ((), ()))
NT = (((1,), (1,)), ((), ()))

VMEM = pl.BlockSpec(memory_space=pltpu.VMEM)
ANY = pl.BlockSpec(memory_space=pl.ANY)
HBM = pl.BlockSpec(memory_space=pltpu.HBM)


def dot(left, right, dims):
    return lax.dot_general(left, right, dims, preferred_element_type=jnp.float32)


class Place:
    def __init__(self, apart):
        split = lax.axis_size("kvh")
        self.shard = lax.axis_index("seq")
        self.first = self.shard < apart
        self.member = lax.rem(self.shard, apart) * split + lax.axis_index("kvh")


def side_by_side(x):
    return jnp.concatenate([x[:, :HEAD_DIM].T, x[:, HEAD_DIM:].T], 1)


def attention_kernel(
    apart, taken, pieces, *refs
):
    place = Place(apart)
    qo_hbm, (halo_hbm, own_hbm, *refs) = refs[:taken], refs[taken:]
    ao_hbm, (dhalo_hbm, down_hbm, *refs) = refs[:pieces], refs[pieces:]
    (kv, qo, ao, dhalo, keys_t, values_t, acc_k, acc_v, exps0, exps1, scores0, scores1, tops, in_sem, q_sem, out_sem) = refs
    rows = qo.shape[0]
    blocks = rows // BLOCK
    whole = WINDOW // BLOCK
    exps, scores = (exps0, exps1), (scores0, scores1)

    def at(i):
        return pl.ds(pl.multiple_of(i * BLOCK, BLOCK), BLOCK)

    def chunks_of(i, near):
        return i + 1 if near else CHUNKS

    def span(i, near):
        start = WINDOW if near else pl.multiple_of(i * BLOCK, BLOCK)
        return pl.ds(start, chunks_of(i, near) * BLOCK)

    def qo_copy(i, piece=0):
        source = qo_hbm[0].at[at(i)] if taken == 1 else qo_hbm[piece]
        return pltpu.make_async_copy(source, qo.at[at(i)], q_sem.at[i])

    def ao_copy(i):
        return pltpu.make_async_copy(ao.at[at(i)], ao_hbm[0].at[at(i)], out_sem.at[0, i])

    def piece_copy(j):
        return pltpu.make_async_copy(ao.at[at(place.member ^ j)], ao_hbm[j], out_sem.at[0, j])

    def dhalo_copy(i):
        return pltpu.make_async_copy(dhalo.at[at(i)], dhalo_hbm.at[at(i)], out_sem.at[1, i])

    halo_copy = pltpu.make_async_copy(halo_hbm, kv.at[pl.ds(0, WINDOW)], in_sem.at[0])
    own_copy = pltpu.make_async_copy(own_hbm, kv.at[pl.ds(WINDOW, rows)], in_sem.at[1])
    halo_copy.start()
    own_copy.start()
    for i in range(blocks):
        (qo_copy(i) if taken == 1 else qo_copy(place.member ^ i, i)).start()

    ones_row = lax.broadcasted_iota(jnp.int32, (ONES, values_t.shape[1]), 0) == 0
    values_t[HEAD_DIM:, :] = jnp.where(ones_row, 1.0, 0.0).astype(jnp.bfloat16)
    acc_k[:, : WINDOW + BLOCK] = jnp.zeros((HEAD_DIM, WINDOW + BLOCK), jnp.float32)
    acc_v[:, : WINDOW + BLOCK] = jnp.zeros((HEAD_DIM, WINDOW + BLOCK), jnp.float32)
    key_at = lax.broadcasted_iota(jnp.int32, (BLOCK, 2 * BLOCK), 0)
    query_at = lax.broadcasted_iota(jnp.int32, (BLOCK, 2 * BLOCK), 1) & (BLOCK - 1)
    def turn(c):
        keys_t[:, at(c)] = kv[at(c), :HEAD_DIM].T
        values_t[:HEAD_DIM, at(c)] = kv[at(c), HEAD_DIM:].T

    def score_dot(i, near):
        return dot(kv[span(i, near), :HEAD_DIM], side_by_side(qo[at(i), :PAIR]), NN)

    def keep_scores(slot, i, found, near):
        top = None
        count = chunks_of(i, near)
        for c in range(count):
            part = found[c * BLOCK : (c + 1) * BLOCK]
            if c == 0 and not near:
                part = jnp.where(key_at > query_at, part, EXCLUDED)
            if c == count - 1:
                part = jnp.where(key_at <= query_at, part, EXCLUDED)
            scores[slot][c * BLOCK : (c + 1) * BLOCK] = part
            high = jnp.max(part, axis=0, keepdims=True)
            top = high if top is None else jnp.maximum(top, high)
        tops[slot, :1] = top * EXP2_SCALE

    def exponentials(slot, i, near):
        top = tops[slot, :1]
        for c in range(chunks_of(i, near)):
            part = slice(c * BLOCK, (c + 1) * BLOCK)
            exps[slot][part] = jnp.exp2(scores[slot][part] * EXP2_SCALE - top).astype(jnp.bfloat16)

    def attended_of(slot, i, o_t, low, near):
        out = dot(values_t[:, span(i, near)], low, NN)
        inverse = 1.0 / out[HEAD_DIM : HEAD_DIM + 1]
        out = out[:HEAD_DIM] * inverse
        grad_out = o_t.astype(jnp.float32)
        delta = jnp.sum(out * grad_out, axis=0, keepdims=True)
        out = out.astype(jnp.bfloat16)
        ao[at(i), :HEAD_DIM] = out[:, :BLOCK].T
        ao[at(i), HEAD_DIM:PAIR] = out[:, BLOCK:].T
        return inverse, delta, (grad_out * inverse).astype(jnp.bfloat16)

    def score_gradients(slot, i, grad_weights, delta, near):
        grad_scores = []
        for c in range(chunks_of(i, near)):
            part = slice(c * BLOCK, (c + 1) * BLOCK)
            grad_scores.append(
                (exps[slot][part].astype(jnp.float32) * (grad_weights[part] - delta)).astype(jnp.bfloat16)
            )
        return jnp.concatenate(grad_scores, 0)

    def spend(i, grad_scores, inverse, near):
        q_t = side_by_side(qo[at(i), :PAIR])
        q_scaled = (q_t.astype(jnp.float32) * inverse).astype(jnp.bfloat16)
        grad_q = (dot(keys_t[:, span(i, near)], grad_scores, NN) * (inverse * SCORE_SCALE)).astype(jnp.bfloat16)
        ao[at(i), PAIR : PAIR + HEAD_DIM] = grad_q[:, :BLOCK].T
        ao[at(i), PAIR + HEAD_DIM :] = grad_q[:, BLOCK:].T
        acc_k[:, span(i, near)] += dot(q_scaled, grad_scores, NT)

    def flush(i):
        dhalo[at(i), :HEAD_DIM] = (acc_k[:, at(i)] * SCORE_SCALE).astype(jnp.bfloat16).T
        dhalo[at(i), HEAD_DIM:] = acc_v[:, at(i)].astype(jnp.bfloat16).T

    def stages(n, slot, begin=True, middle=True, end=True, near=False):
        if end:
            o_t = side_by_side(qo[at(n - 2), PAIR:])
            low = exps[slot][: chunks_of(n - 2, near) * BLOCK]
            inverse, delta, o_scaled = attended_of(slot, n - 2, o_t, low, near)
            grad_weights = dot(kv[span(n - 2, near), HEAD_DIM:], o_t, NN)
        if begin:
            found = score_dot(n, near)
        if end:
            grad_scores = score_gradients(slot, n - 2, grad_weights, delta, near)
            acc_v[:, span(n - 2, near)] += dot(o_scaled, low, NT)
        if middle:
            exponentials(1 - slot, n - 1, near)
        if begin:
            keep_scores(slot, n, found, near)
        if end:
            spend(n - 2, grad_scores, inverse, near)
            if not near:
                flush(n - 2)

    def extend(c):
        turn(c)
        acc_k[:, at(c)] = jnp.zeros((HEAD_DIM, BLOCK), jnp.float32)
        acc_v[:, at(c)] = jnp.zeros((HEAD_DIM, BLOCK), jnp.float32)

    def send(i):
        dhalo_copy(i).start()
        if pieces == 1:
            ao_copy(i).start()

    halo_copy.wait()
    own_copy.wait()
    qo_copy(0).wait()
    qo_copy(1).wait()

    @pl.when(jnp.logical_not(place.first))
    def _():
        stages(0, 0, middle=False, end=False)
        stages(1, 1, end=False)
        for c in range(whole + 1):
            turn(c)

        def step(j, carry):
            n = 2 * j
            qo_copy(n).wait()
            qo_copy(n + 1).wait()
            stages(n, 0)
            extend(n + whole - 1)
            stages(n + 1, 1)
            extend(n + whole)
            send(n - 2)
            send(n - 1)
            return carry

        lax.fori_loop(1, blocks // 2, step, 0)
        stages(blocks, 0, begin=False)
        extend(blocks + whole - 1)
        send(blocks - 2)
        stages(blocks + 1, 1, begin=False, middle=False)
        send(blocks - 1)

    @pl.when(place.first)
    def _():
        dhalo[...] = jnp.zeros_like(dhalo)
        for n in range(blocks + 2):
            if 2 <= n < blocks:
                qo_copy(n).wait()
            if n >= 2:
                extend(whole + n - 2)
            stages(n, n % 2, n < blocks, 1 <= n <= blocks, n >= 2, near=True)
            if n >= 2:
                send(n - 2)

    if pieces > 1:
        for j in range(pieces):
            piece_copy(j).start()
    own_k = pltpu.make_async_copy(acc_k.at[:, pl.ds(WINDOW, rows)], down_hbm.at[0], in_sem.at[0])
    own_v = pltpu.make_async_copy(acc_v.at[:, pl.ds(WINDOW, rows)], down_hbm.at[1], in_sem.at[1])
    own_k.start()
    own_v.start()
    for i in range(blocks):
        (ao_copy(i) if pieces == 1 else piece_copy(i)).wait()
        dhalo_copy(i).wait()
    own_k.wait()
    own_v.wait()


def attention(apart, qo, halo, own, pieces):
    rows = own.shape[0]
    blocks = rows // BLOCK
    reach = WINDOW + rows
    bf16, f32 = jnp.bfloat16, jnp.float32
    width = 2 * PAIR
    return pl.pallas_call(
        functools.partial(attention_kernel, apart, len(qo), pieces),
        out_shape=(
            *[jax.ShapeDtypeStruct((rows // pieces, width), bf16)] * pieces,
            jax.ShapeDtypeStruct(halo.shape, bf16),
            jax.ShapeDtypeStruct((2, HEAD_DIM, rows), f32),
        ),
        in_specs=[ANY] * (len(qo) + 2),
        out_specs=(HBM,) * (pieces + 2),
        scratch_shapes=[
            pltpu.VMEM((reach, PAIR), bf16),
            pltpu.VMEM((rows, 2 * PAIR), bf16),
            pltpu.VMEM((rows, width), bf16),
            pltpu.VMEM(halo.shape, bf16),
            pltpu.VMEM((HEAD_DIM, reach + BLOCK), bf16),
            pltpu.VMEM((HEAD_DIM + ONES, reach + BLOCK), bf16),
            pltpu.VMEM((HEAD_DIM, reach + BLOCK), f32),
            pltpu.VMEM((HEAD_DIM, reach + BLOCK), f32),
            pltpu.VMEM((CHUNKS * BLOCK, 2 * BLOCK), bf16),
            pltpu.VMEM((CHUNKS * BLOCK, 2 * BLOCK), bf16),
            pltpu.VMEM((CHUNKS * BLOCK, 2 * BLOCK), f32),
            pltpu.VMEM((CHUNKS * BLOCK, 2 * BLOCK), f32),
            pltpu.VMEM((2, 8, 2 * BLOCK), f32),
            pltpu.SemaphoreType.DMA((2,)),
            pltpu.SemaphoreType.DMA((blocks,)),
            pltpu.SemaphoreType.DMA((2, blocks)),
        ],
        compiler_params=pltpu.CompilerParams(vmem_limit_bytes=58 * 2**20),
        cost_estimate=pl.CostEstimate(flops=10**10, bytes_accessed=4 * 2**20, transcendentals=0),
        name="attention",
    )(*qo, halo, own)


def interleave_kernel(apart, width, sets, *refs):
    place = Place(apart)
    arrays, refs = refs[:2], refs[2:]
    groups = arrays[0].shape[1] // sets[0][1][0][2]
    outs, refs = refs[: -(4 + len(sets))], refs[-(4 + len(sets)) :]
    fetched, staged, (in_sem, out_sem) = refs[:2], refs[2:-2], refs[-2:]
    loads = [pltpu.make_async_copy(arrays[n], fetched[n], in_sem.at[n]) for n in range(2)]
    for load in loads:
        load.start()
    for load in loads:
        load.wait()
    stores = []
    taken = 0
    for k, (split, parts) in enumerate(sets):
        for g in range(groups):
            source = place.member ^ g if split else g
            for n, (which, start, stride) in enumerate(parts):
                at = source * stride + start
                if split:
                    at = pl.multiple_of(at, HEAD_DIM)
                staged[k][g, :, n * width : (n + 1) * width] = fetched[which][:, pl.ds(at, width)]
            out = outs[taken + g] if split else outs[taken].at[g]
            stores.append(pltpu.make_async_copy(staged[k].at[g], out, out_sem.at[k, g]))
            stores[-1].start()
        taken += groups if split else 1
    for store in stores:
        store.wait()


def interleave(apart, arrays, groups, width, sets):
    rows, cols = arrays[0].shape
    dtype = arrays[0].dtype
    shapes, staged = [], []
    for split, parts in sets:
        whole = (groups, rows, width * len(parts))
        staged.append(pltpu.VMEM(whole, dtype))
        shapes += [jax.ShapeDtypeStruct(whole[1:], dtype)] * groups if split else [jax.ShapeDtypeStruct(whole, dtype)]
    return pl.pallas_call(
        functools.partial(interleave_kernel, apart, width, sets),
        out_shape=tuple(shapes),
        in_specs=[HBM, HBM],
        out_specs=(HBM,) * len(shapes),
        scratch_shapes=[
            pltpu.VMEM((rows, cols), dtype),
            pltpu.VMEM((rows, cols), dtype),
            *staged,
            pltpu.SemaphoreType.DMA((2,)),
            pltpu.SemaphoreType.DMA((len(sets), groups)),
        ],
        compiler_params=pltpu.CompilerParams(vmem_limit_bytes=58 * 2**20),
        name="interleave",
    )(*arrays)


def assemble_kernel(apart, *refs):
    place = Place(apart)
    *arrays, sem = refs
    count, heads = sem.shape
    pieces, outs = arrays[:count], arrays[count:]
    rows, width = pieces[0].shape[0], outs[0].shape[1]
    copies = []
    for j in range(count):
        at = pl.ds(pl.multiple_of((place.member ^ j) * rows, BLOCK), rows)
        for h in range(heads):
            source = pieces[j].at[:, pl.ds(h * width, width)]
            copies.append(pltpu.make_async_copy(source, outs[h].at[at], sem.at[j, h]))
    for copy in copies:
        copy.start()
    for copy in copies:
        copy.wait()


def assemble(apart, pieces, heads):
    rows, width = pieces[0].shape
    shape = jax.ShapeDtypeStruct((len(pieces) * rows, width // heads), pieces[0].dtype)
    return pl.pallas_call(
        functools.partial(assemble_kernel, apart),
        out_shape=(shape,) * heads,
        in_specs=[ANY] * len(pieces),
        out_specs=(VMEM,) * heads,
        scratch_shapes=[pltpu.SemaphoreType.DMA((len(pieces), heads))],
        compiler_params=pltpu.CompilerParams(vmem_limit_bytes=8 * 2**20),
        name="assemble",
    )(*pieces)


def group_at(place, j, width):
    return pl.multiple_of((place.member ^ j) * width, HEAD_DIM)


def spread_kernel(apart, x_ref, *refs):
    place = Place(apart)
    *pieces, a_ref, b_ref = refs
    groups, _, width = x_ref.shape
    half = width // 2
    for g in range(groups):
        a_ref[:, g * width : g * width + half] = x_ref[g, :, :half]
        b_ref[:, g * width : g * width + half] = x_ref[g, :, half:]
        cols = pl.ds(group_at(place, g, width) + half, half)
        a_ref[:, cols] = pieces[g][:, :half]
        b_ref[:, cols] = pieces[g][:, half:]


def spread(apart, x, pieces):
    groups, rows, width = x.shape
    shape = jax.ShapeDtypeStruct((rows, groups * width), x.dtype)
    return pl.pallas_call(
        functools.partial(spread_kernel, apart),
        out_shape=(shape, shape),
        in_specs=[VMEM] * (groups + 1),
        out_specs=(VMEM, VMEM),
        compiler_params=pltpu.CompilerParams(vmem_limit_bytes=16 * 2**20),
        name="spread",
    )(x, *pieces)


def settle_kernel(own0, own1, back0, done_ref, open_ref):
    for n, scale in enumerate((SCORE_SCALE, 1.0)):
        cols = slice(n * HEAD_DIM, (n + 1) * HEAD_DIM)
        for i in range(done_ref.shape[0] // BLOCK):
            at = slice(i * BLOCK, (i + 1) * BLOCK)
            total = (own0[n, :, at] * scale).T + back0[at, cols].astype(jnp.float32)
            done_ref[at, cols] = total.astype(jnp.bfloat16)
            open_ref[at, cols] = (own1[n, :, at] * scale).T


def settle(own, back):
    return pl.pallas_call(
        settle_kernel,
        out_shape=(
            jax.ShapeDtypeStruct(back.shape, jnp.bfloat16),
            jax.ShapeDtypeStruct(back.shape, jnp.float32),
        ),
        in_specs=[VMEM] * 3,
        out_specs=(VMEM,) * 2,
        compiler_params=pltpu.CompilerParams(vmem_limit_bytes=16 * 2**20),
        name="settle",
    )(*own, back)


def add_kernel(apart, done_ref, open_ref, back_ref, *out_refs):
    place = Place(apart)
    rows = out_refs[0].shape[0]
    for j, out_ref in enumerate(out_refs):
        at = pl.ds(group_at(place, j, rows), rows)
        out_ref[:, :PAIR] = done_ref[at, :]
        out_ref[:, PAIR:] = (open_ref[at, :] + back_ref[at, :].astype(jnp.float32)).astype(jnp.bfloat16)


def add(apart, done, started, back, groups):
    rows, width = back.shape
    shape = jax.ShapeDtypeStruct((rows // groups, 2 * width), jnp.bfloat16)
    return pl.pallas_call(
        functools.partial(add_kernel, apart),
        out_shape=(shape,) * groups,
        in_specs=[VMEM] * 3,
        out_specs=(VMEM,) * groups,
        compiler_params=pltpu.CompilerParams(vmem_limit_bytes=16 * 2**20),
        name="add",
    )(done, started, back)


def unpack_kernel(apart, *refs):
    place = Place(apart)
    *pieces, a_ref, b_ref = refs
    heads = pieces[0].shape[1] // PAIR
    for j, piece in enumerate(pieces):
        start = group_at(place, j, heads * HEAD_DIM)
        for h in range(heads):
            cols = pl.ds(start + h * HEAD_DIM, HEAD_DIM)
            a_ref[:, cols] = piece[:, h * PAIR : h * PAIR + HEAD_DIM]
            b_ref[:, cols] = piece[:, h * PAIR + HEAD_DIM : (h + 1) * PAIR]


def unpack(apart, pieces):
    rows, width = pieces[0].shape
    shape = jax.ShapeDtypeStruct((rows, len(pieces) * width // 2), pieces[0].dtype)
    return pl.pallas_call(
        functools.partial(unpack_kernel, apart),
        out_shape=(shape, shape),
        in_specs=[VMEM] * len(pieces),
        out_specs=(VMEM, VMEM),
        compiler_params=pltpu.CompilerParams(vmem_limit_bytes=16 * 2**20),
        name="unpack",
    )(*pieces)


def body(queries, key_rows, value_rows, grad_out):
    shards, split = lax.axis_size("seq"), lax.axis_size("kvh")
    rows = queries.shape[0]
    apart = WINDOW // (rows * split)
    members = apart * split
    heads = key_rows.shape[1] // (members * HEAD_DIM)
    groups = [[g * members + i for i in range(members)] for g in range(shards // apart)]
    def exchange(x):
        return lax.all_to_all(x, ("seq", "kvh"), 0, 0, tiled=True, axis_index_groups=groups)

    order = sorted(range(1, members), key=lambda j: j == 1)

    def swap(pieces, before=None, limit=IN_FLIGHT):
        every = range(shards * split)
        out = [pieces[0]] * members
        sent = [] if before is None else [(before, j) for j in order]
        for j in order:
            piece = pieces[j]
            if len(sent) >= limit:
                box, k = sent[-limit]
                piece, box[k] = lax.optimization_barrier((piece, box[k]))
            out[j] = lax.ppermute(piece, ("seq", "kvh"), [(i, i ^ j) for i in every])
            sent.append((out, j))
        return out

    def onward(x):
        return lax.ppermute(x, "seq", [(i, (i + apart) % shards) for i in range(shards)])

    def backward(x, wrap):
        return lax.ppermute(x, "seq", [((i + apart) % shards, i) for i in range(shards if wrap else shards - apart)])

    stride = heads * HEAD_DIM
    kv_parts = [(n, h * HEAD_DIM, stride) for h in range(heads) for n in range(2)]
    def qo_parts(h):
        return [(n, h * PAIR, 2 * stride) for n in range(2)]

    kv = list(interleave(apart, (key_rows, value_rows), members, HEAD_DIM, [(True, kv_parts)]))
    sets = [(h == 0, qo_parts(h)) for h in range(heads)]
    packed = interleave(apart, (queries, grad_out), members, PAIR, sets)
    late = order[EARLY]
    kv[late], (*first, second) = lax.optimization_barrier((kv[late], packed))
    kv = swap(kv, None, 5)
    first = swap(first, kv, 5)
    own = assemble(apart, kv, heads)
    second, first[order[HOLD]] = lax.optimization_barrier((second, first[order[HOLD]]))
    qos = [first, [exchange(second).reshape(WINDOW, -1)]]
    held, first[order[-2]] = lax.optimization_barrier((own[1], first[order[-2]]))
    halos = [onward(own[0]), onward(held)]
    outs, mine, back = [], [], []
    for h in range(heads):
        last = h == heads - 1
        *ao, dhalo, down = attention(apart, qos[h], halos[h], own[h], members if last else 1)
        if last:
            ao[order[WAITS]], back[h - 1] = lax.optimization_barrier((ao[order[WAITS]], back[h - 1]))
        back.append(backward(dhalo, not last))
        outs.append(swap(ao) if last else exchange(ao[0].reshape(members, rows, -1)))
        mine.append(down)
    total = add(apart, *settle(mine, back[0]), back[1], members)
    outs[0], total = lax.optimization_barrier((outs[0], total))
    grad_k, grad_v = unpack(apart, swap(total, outs[-1], 5))
    attended, grad_q = spread(apart, *outs)
    return (attended, grad_q, grad_k, grad_v)


def solution(mesh):
    placed = P(("seq", "kvh"), None)
    return jax.shard_map(
        body, mesh=mesh, in_specs=(placed,) * 4, out_specs=(placed,) * 4, check_vma=False
    )
```

```python
import functools

import jax
import jax.numpy as jnp
from jax import lax
from jax.experimental import pallas as pl
from jax.experimental.pallas import tpu as pltpu
from jax.sharding import PartitionSpec as P

HEAD_DIM = 128
PAIR = 2 * HEAD_DIM
WINDOW = 1024
BLOCK = 128
CHUNKS = WINDOW // BLOCK + 1
SCORE_SCALE = 168.0 ** (-0.5)
EXP2_SCALE = SCORE_SCALE * 1.4426950408889634
EXCLUDED = -1e30
ONES = 16
IN_FLIGHT = 4
HOLD = 3
WAITS = 5
EARLY = 4

NN = (((1,), (0,)), ((), ()))
NT = (((1,), (1,)), ((), ()))

VMEM = pl.BlockSpec(memory_space=pltpu.VMEM)
ANY = pl.BlockSpec(memory_space=pl.ANY)
HBM = pl.BlockSpec(memory_space=pltpu.HBM)


def dot(left, right, dims):
    return lax.dot_general(left, right, dims, preferred_element_type=jnp.float32)


class Place:
    def __init__(self, apart):
        split = lax.axis_size("kvh")
        self.shard = lax.axis_index("seq")
        self.first = self.shard < apart
        self.member = lax.rem(self.shard, apart) * split + lax.axis_index("kvh")


def side_by_side(x):
    return jnp.concatenate([x[:, :HEAD_DIM].T, x[:, HEAD_DIM:].T], 1)


def attention_kernel(
    apart, taken, pieces, *refs
):
    place = Place(apart)
    qo_hbm, (halo_hbm, own_hbm, *refs) = refs[:taken], refs[taken:]
    ao_hbm, (dhalo_hbm, down_hbm, *refs) = refs[:pieces], refs[pieces:]
    (kv, qo, ao, dhalo, keys_t, values_t, acc_k, acc_v, exps0, exps1, scores0, scores1, tops, in_sem, q_sem, out_sem) = refs
    rows = qo.shape[0]
    blocks = rows // BLOCK
    whole = WINDOW // BLOCK
    exps, scores = (exps0, exps1), (scores0, scores1)

    def at(i):
        return pl.ds(pl.multiple_of(i * BLOCK, BLOCK), BLOCK)

    def chunks_of(i, near):
        return i + 1 if near else CHUNKS

    def span(i, near):
        start = WINDOW if near else pl.multiple_of(i * BLOCK, BLOCK)
        return pl.ds(start, chunks_of(i, near) * BLOCK)

    def qo_copy(i, piece=0):
        source = qo_hbm[0].at[at(i)] if taken == 1 else qo_hbm[piece]
        return pltpu.make_async_copy(source, qo.at[at(i)], q_sem.at[i])

    def ao_copy(i):
        return pltpu.make_async_copy(ao.at[at(i)], ao_hbm[0].at[at(i)], out_sem.at[0, i])

    def piece_copy(j):
        return pltpu.make_async_copy(ao.at[at(place.member ^ j)], ao_hbm[j], out_sem.at[0, j])

    def dhalo_copy(i):
        return pltpu.make_async_copy(dhalo.at[at(i)], dhalo_hbm.at[at(i)], out_sem.at[1, i])

    halo_copy = pltpu.make_async_copy(halo_hbm, kv.at[pl.ds(0, WINDOW)], in_sem.at[0])
    own_copy = pltpu.make_async_copy(own_hbm, kv.at[pl.ds(WINDOW, rows)], in_sem.at[1])
    halo_copy.start()
    own_copy.start()
    for i in range(blocks):
        (qo_copy(i) if taken == 1 else qo_copy(place.member ^ i, i)).start()

    ones_row = lax.broadcasted_iota(jnp.int32, (ONES, values_t.shape[1]), 0) == 0
    values_t[HEAD_DIM:, :] = jnp.where(ones_row, 1.0, 0.0).astype(jnp.bfloat16)
    acc_k[:, : WINDOW + BLOCK] = jnp.zeros((HEAD_DIM, WINDOW + BLOCK), jnp.float32)
    acc_v[:, : WINDOW + BLOCK] = jnp.zeros((HEAD_DIM, WINDOW + BLOCK), jnp.float32)
    key_at = lax.broadcasted_iota(jnp.int32, (BLOCK, 2 * BLOCK), 0)
    query_at = lax.broadcasted_iota(jnp.int32, (BLOCK, 2 * BLOCK), 1) & (BLOCK - 1)
    def turn(c):
        keys_t[:, at(c)] = kv[at(c), :HEAD_DIM].T
        values_t[:HEAD_DIM, at(c)] = kv[at(c), HEAD_DIM:].T

    def score_dot(i, near):
        return dot(kv[span(i, near), :HEAD_DIM], side_by_side(qo[at(i), :PAIR]), NN)

    def keep_scores(slot, i, found, near):
        top = None
        count = chunks_of(i, near)
        for c in range(count):
            part = found[c * BLOCK : (c + 1) * BLOCK]
            if c == 0 and not near:
                part = jnp.where(key_at > query_at, part, EXCLUDED)
            if c == count - 1:
                part = jnp.where(key_at <= query_at, part, EXCLUDED)
            scores[slot][c * BLOCK : (c + 1) * BLOCK] = part
            high = jnp.max(part, axis=0, keepdims=True)
            top = high if top is None else jnp.maximum(top, high)
        tops[slot, :1] = top * EXP2_SCALE

    def exponentials(slot, i, near):
        top = tops[slot, :1]
        for c in range(chunks_of(i, near)):
            part = slice(c * BLOCK, (c + 1) * BLOCK)
            exps[slot][part] = jnp.exp2(scores[slot][part] * EXP2_SCALE - top).astype(jnp.bfloat16)

    def attended_of(slot, i, o_t, low, near):
        out = dot(values_t[:, span(i, near)], low, NN)
        inverse = 1.0 / out[HEAD_DIM : HEAD_DIM + 1]
        out = out[:HEAD_DIM] * inverse
        grad_out = o_t.astype(jnp.float32)
        delta = jnp.sum(out * grad_out, axis=0, keepdims=True)
        out = out.astype(jnp.bfloat16)
        ao[at(i), :HEAD_DIM] = out[:, :BLOCK].T
        ao[at(i), HEAD_DIM:PAIR] = out[:, BLOCK:].T
        return inverse, delta, (grad_out * inverse).astype(jnp.bfloat16)

    def score_gradients(slot, i, grad_weights, delta, near):
        grad_scores = []
        for c in range(chunks_of(i, near)):
            part = slice(c * BLOCK, (c + 1) * BLOCK)
            grad_scores.append(
                (exps[slot][part].astype(jnp.float32) * (grad_weights[part] - delta)).astype(jnp.bfloat16)
            )
        return jnp.concatenate(grad_scores, 0)

    def spend(i, grad_scores, inverse, near):
        q_t = side_by_side(qo[at(i), :PAIR])
        q_scaled = (q_t.astype(jnp.float32) * inverse).astype(jnp.bfloat16)
        grad_q = (dot(keys_t[:, span(i, near)], grad_scores, NN) * (inverse * SCORE_SCALE)).astype(jnp.bfloat16)
        ao[at(i), PAIR : PAIR + HEAD_DIM] = grad_q[:, :BLOCK].T
        ao[at(i), PAIR + HEAD_DIM :] = grad_q[:, BLOCK:].T
        acc_k[:, span(i, near)] += dot(q_scaled, grad_scores, NT)

    def flush(i):
        dhalo[at(i), :HEAD_DIM] = (acc_k[:, at(i)] * SCORE_SCALE).astype(jnp.bfloat16).T
        dhalo[at(i), HEAD_DIM:] = acc_v[:, at(i)].astype(jnp.bfloat16).T

    def stages(n, slot, begin=True, middle=True, end=True, near=False):
        if end:
            o_t = side_by_side(qo[at(n - 2), PAIR:])
            low = exps[slot][: chunks_of(n - 2, near) * BLOCK]
            inverse, delta, o_scaled = attended_of(slot, n - 2, o_t, low, near)
            grad_weights = dot(kv[span(n - 2, near), HEAD_DIM:], o_t, NN)
        if begin:
            found = score_dot(n, near)
        if end:
            grad_scores = score_gradients(slot, n - 2, grad_weights, delta, near)
            acc_v[:, span(n - 2, near)] += dot(o_scaled, low, NT)
        if middle:
            exponentials(1 - slot, n - 1, near)
        if begin:
            keep_scores(slot, n, found, near)
        if end:
            spend(n - 2, grad_scores, inverse, near)
            if not near:
                flush(n - 2)

    def extend(c):
        turn(c)
        acc_k[:, at(c)] = jnp.zeros((HEAD_DIM, BLOCK), jnp.float32)
        acc_v[:, at(c)] = jnp.zeros((HEAD_DIM, BLOCK), jnp.float32)

    def send(i):
        dhalo_copy(i).start()
        if pieces == 1:
            ao_copy(i).start()

    halo_copy.wait()
    own_copy.wait()
    qo_copy(0).wait()
    qo_copy(1).wait()

    @pl.when(jnp.logical_not(place.first))
    def _():
        stages(0, 0, middle=False, end=False)
        stages(1, 1, end=False)
        for c in range(whole + 1):
            turn(c)

        def step(j, carry):
            n = 2 * j
            qo_copy(n).wait()
            qo_copy(n + 1).wait()
            stages(n, 0)
            extend(n + whole - 1)
            stages(n + 1, 1)
            extend(n + whole)
            send(n - 2)
            send(n - 1)
            return carry

        lax.fori_loop(1, blocks // 2, step, 0)
        stages(blocks, 0, begin=False)
        extend(blocks + whole - 1)
        send(blocks - 2)
        stages(blocks + 1, 1, begin=False, middle=False)
        send(blocks - 1)

    @pl.when(place.first)
    def _():
        dhalo[...] = jnp.zeros_like(dhalo)
        for n in range(blocks + 2):
            if 2 <= n < blocks:
                qo_copy(n).wait()
            if n >= 2:
                extend(whole + n - 2)
            stages(n, n % 2, n < blocks, 1 <= n <= blocks, n >= 2, near=True)
            if n >= 2:
                send(n - 2)

    if pieces > 1:
        for j in range(pieces):
            piece_copy(j).start()
    own_k = pltpu.make_async_copy(acc_k.at[:, pl.ds(WINDOW, rows)], down_hbm.at[0], in_sem.at[0])
    own_v = pltpu.make_async_copy(acc_v.at[:, pl.ds(WINDOW, rows)], down_hbm.at[1], in_sem.at[1])
    own_k.start()
    own_v.start()
    for i in range(blocks):
        (ao_copy(i) if pieces == 1 else piece_copy(i)).wait()
        dhalo_copy(i).wait()
    own_k.wait()
    own_v.wait()


def attention(apart, qo, halo, own, pieces):
    rows = own.shape[0]
    blocks = rows // BLOCK
    reach = WINDOW + rows
    bf16, f32 = jnp.bfloat16, jnp.float32
    width = 2 * PAIR
    return pl.pallas_call(
        functools.partial(attention_kernel, apart, len(qo), pieces),
        out_shape=(
            *[jax.ShapeDtypeStruct((rows // pieces, width), bf16)] * pieces,
            jax.ShapeDtypeStruct(halo.shape, bf16),
            jax.ShapeDtypeStruct((2, HEAD_DIM, rows), f32),
        ),
        in_specs=[ANY] * (len(qo) + 2),
        out_specs=(HBM,) * (pieces + 2),
        scratch_shapes=[
            pltpu.VMEM((reach, PAIR), bf16),
            pltpu.VMEM((rows, 2 * PAIR), bf16),
            pltpu.VMEM((rows, width), bf16),
            pltpu.VMEM(halo.shape, bf16),
            pltpu.VMEM((HEAD_DIM, reach + BLOCK), bf16),
            pltpu.VMEM((HEAD_DIM + ONES, reach + BLOCK), bf16),
            pltpu.VMEM((HEAD_DIM, reach + BLOCK), f32),
            pltpu.VMEM((HEAD_DIM, reach + BLOCK), f32),
            pltpu.VMEM((CHUNKS * BLOCK, 2 * BLOCK), bf16),
            pltpu.VMEM((CHUNKS * BLOCK, 2 * BLOCK), bf16),
            pltpu.VMEM((CHUNKS * BLOCK, 2 * BLOCK), f32),
            pltpu.VMEM((CHUNKS * BLOCK, 2 * BLOCK), f32),
            pltpu.VMEM((2, 8, 2 * BLOCK), f32),
            pltpu.SemaphoreType.DMA((2,)),
            pltpu.SemaphoreType.DMA((blocks,)),
            pltpu.SemaphoreType.DMA((2, blocks)),
        ],
        compiler_params=pltpu.CompilerParams(vmem_limit_bytes=58 * 2**20),
        cost_estimate=pl.CostEstimate(flops=10**10, bytes_accessed=4 * 2**20, transcendentals=0),
        name="attention",
    )(*qo, halo, own)


def interleave_kernel(apart, width, sets, *refs):
    place = Place(apart)
    arrays, refs = refs[:2], refs[2:]
    groups = arrays[0].shape[1] // sets[0][1][0][2]
    outs, refs = refs[: -(4 + len(sets))], refs[-(4 + len(sets)) :]
    fetched, staged, (in_sem, out_sem) = refs[:2], refs[2:-2], refs[-2:]
    loads = [pltpu.make_async_copy(arrays[n], fetched[n], in_sem.at[n]) for n in range(2)]
    for load in loads:
        load.start()
    arrived = set()
    stores = []
    taken = 0
    for k, (split, parts) in enumerate(sets):
        to = 0
        for which, start, stride, *size in parts:
            span = size[0] if size else width
            if which not in arrived:
                loads[which].wait()
                arrived.add(which)
            for g in range(groups):
                at = (place.member ^ g if split else g) * stride + start
                if split:
                    at = pl.multiple_of(at, HEAD_DIM)
                staged[k][g, :, to : to + span] = fetched[which][:, pl.ds(at, span)]
            to += span
        for g in range(groups):
            out = outs[taken + g] if split else outs[taken].at[g]
            stores.append(pltpu.make_async_copy(staged[k].at[g], out, out_sem.at[k, g]))
            stores[-1].start()
        taken += groups if split else 1
    for store in stores:
        store.wait()


def interleave(apart, arrays, groups, width, sets):
    rows, cols = arrays[0].shape
    dtype = arrays[0].dtype
    shapes, staged = [], []
    for split, parts in sets:
        whole = (groups, rows, width * len(parts))
        staged.append(pltpu.VMEM(whole, dtype))
        shapes += [jax.ShapeDtypeStruct(whole[1:], dtype)] * groups if split else [jax.ShapeDtypeStruct(whole, dtype)]
    return pl.pallas_call(
        functools.partial(interleave_kernel, apart, width, sets),
        out_shape=tuple(shapes),
        in_specs=[HBM, HBM],
        out_specs=(HBM,) * len(shapes),
        scratch_shapes=[
            pltpu.VMEM((rows, cols), dtype),
            pltpu.VMEM((rows, cols), dtype),
            *staged,
            pltpu.SemaphoreType.DMA((2,)),
            pltpu.SemaphoreType.DMA((len(sets), groups)),
        ],
        compiler_params=pltpu.CompilerParams(vmem_limit_bytes=58 * 2**20),
        name="interleave",
    )(*arrays)


def assemble_kernel(apart, *refs):
    place = Place(apart)
    *arrays, sem = refs
    count, heads = sem.shape
    pieces, outs = arrays[:count], arrays[count:]
    rows, width = pieces[0].shape[0], outs[0].shape[1]
    copies = []
    for j in range(count):
        at = pl.ds(pl.multiple_of((place.member ^ j) * rows, BLOCK), rows)
        for h in range(heads):
            source = pieces[j].at[:, pl.ds(h * width, width)]
            copies.append(pltpu.make_async_copy(source, outs[h].at[at], sem.at[j, h]))
    for copy in copies:
        copy.start()
    for copy in copies:
        copy.wait()


def assemble(apart, pieces, heads):
    rows, width = pieces[0].shape
    shape = jax.ShapeDtypeStruct((len(pieces) * rows, width // heads), pieces[0].dtype)
    return pl.pallas_call(
        functools.partial(assemble_kernel, apart),
        out_shape=(shape,) * heads,
        in_specs=[ANY] * len(pieces),
        out_specs=(VMEM,) * heads,
        scratch_shapes=[pltpu.SemaphoreType.DMA((len(pieces), heads))],
        compiler_params=pltpu.CompilerParams(vmem_limit_bytes=8 * 2**20),
        name="assemble",
    )(*pieces)


def group_at(place, j, width):
    return pl.multiple_of((place.member ^ j) * width, HEAD_DIM)


def spread_kernel(apart, x_ref, *refs):
    place = Place(apart)
    *pieces, a_ref, b_ref = refs
    groups, _, width = x_ref.shape
    half = width // 2
    for g in range(groups):
        a_ref[:, g * width : g * width + half] = x_ref[g, :, :half]
        b_ref[:, g * width : g * width + half] = x_ref[g, :, half:]
        cols = pl.ds(group_at(place, g, width) + half, half)
        a_ref[:, cols] = pieces[g][:, :half]
        b_ref[:, cols] = pieces[g][:, half:]


def spread(apart, x, pieces):
    groups, rows, width = x.shape
    shape = jax.ShapeDtypeStruct((rows, groups * width), x.dtype)
    return pl.pallas_call(
        functools.partial(spread_kernel, apart),
        out_shape=(shape, shape),
        in_specs=[VMEM] * (groups + 1),
        out_specs=(VMEM, VMEM),
        compiler_params=pltpu.CompilerParams(vmem_limit_bytes=16 * 2**20),
        name="spread",
    )(x, *pieces)


def settle_kernel(own0, own1, back0, done_ref, open_ref):
    for n, scale in enumerate((SCORE_SCALE, 1.0)):
        cols = slice(n * HEAD_DIM, (n + 1) * HEAD_DIM)
        for i in range(done_ref.shape[0] // BLOCK):
            at = slice(i * BLOCK, (i + 1) * BLOCK)
            total = (own0[n, :, at] * scale).T + back0[at, cols].astype(jnp.float32)
            done_ref[at, cols] = total.astype(jnp.bfloat16)
            open_ref[at, cols] = (own1[n, :, at] * scale).T


def settle(own, back):
    return pl.pallas_call(
        settle_kernel,
        out_shape=(
            jax.ShapeDtypeStruct(back.shape, jnp.bfloat16),
            jax.ShapeDtypeStruct(back.shape, jnp.float32),
        ),
        in_specs=[VMEM] * 3,
        out_specs=(VMEM,) * 2,
        compiler_params=pltpu.CompilerParams(vmem_limit_bytes=16 * 2**20),
        name="settle",
    )(*own, back)


def add_kernel(apart, done_ref, open_ref, back_ref, *out_refs):
    place = Place(apart)
    rows = out_refs[0].shape[0]
    for j, out_ref in enumerate(out_refs):
        at = pl.ds(group_at(place, j, rows), rows)
        out_ref[:, :PAIR] = done_ref[at, :]
        out_ref[:, PAIR:] = (open_ref[at, :] + back_ref[at, :].astype(jnp.float32)).astype(jnp.bfloat16)


def add(apart, done, started, back, groups):
    rows, width = back.shape
    shape = jax.ShapeDtypeStruct((rows // groups, 2 * width), jnp.bfloat16)
    return pl.pallas_call(
        functools.partial(add_kernel, apart),
        out_shape=(shape,) * groups,
        in_specs=[VMEM] * 3,
        out_specs=(VMEM,) * groups,
        compiler_params=pltpu.CompilerParams(vmem_limit_bytes=16 * 2**20),
        name="add",
    )(done, started, back)


def unpack_kernel(apart, *refs):
    place = Place(apart)
    *pieces, a_ref, b_ref = refs
    heads = pieces[0].shape[1] // PAIR
    for j, piece in enumerate(pieces):
        start = group_at(place, j, heads * HEAD_DIM)
        for h in range(heads):
            cols = pl.ds(start + h * HEAD_DIM, HEAD_DIM)
            a_ref[:, cols] = piece[:, h * PAIR : h * PAIR + HEAD_DIM]
            b_ref[:, cols] = piece[:, h * PAIR + HEAD_DIM : (h + 1) * PAIR]


def unpack(apart, pieces):
    rows, width = pieces[0].shape
    shape = jax.ShapeDtypeStruct((rows, len(pieces) * width // 2), pieces[0].dtype)
    return pl.pallas_call(
        functools.partial(unpack_kernel, apart),
        out_shape=(shape, shape),
        in_specs=[VMEM] * len(pieces),
        out_specs=(VMEM, VMEM),
        compiler_params=pltpu.CompilerParams(vmem_limit_bytes=16 * 2**20),
        name="unpack",
    )(*pieces)


def body(queries, key_rows, value_rows, grad_out):
    shards, split = lax.axis_size("seq"), lax.axis_size("kvh")
    rows = queries.shape[0]
    apart = WINDOW // (rows * split)
    members = apart * split
    heads = key_rows.shape[1] // (members * HEAD_DIM)
    groups = [[g * members + i for i in range(members)] for g in range(shards // apart)]
    def exchange(x):
        return lax.all_to_all(x, ("seq", "kvh"), 0, 0, tiled=True, axis_index_groups=groups)

    order = sorted(range(1, members), key=lambda j: j == 1)

    def swap(pieces, before=None, limit=IN_FLIGHT):
        every = range(shards * split)
        out = [pieces[0]] * members
        sent = [] if before is None else [(before, j) for j in order]
        for j in order:
            piece = pieces[j]
            if len(sent) >= limit:
                box, k = sent[-limit]
                piece, box[k] = lax.optimization_barrier((piece, box[k]))
            out[j] = lax.ppermute(piece, ("seq", "kvh"), [(i, i ^ j) for i in every])
            sent.append((out, j))
        return out

    def onward(x):
        return lax.ppermute(x, "seq", [(i, (i + apart) % shards) for i in range(shards)])

    def backward(x, wrap):
        return lax.ppermute(x, "seq", [((i + apart) % shards, i) for i in range(shards if wrap else shards - apart)])

    stride = heads * HEAD_DIM
    kv_parts = [(n, h * HEAD_DIM, stride) for h in range(heads) for n in range(2)]
    def qo_parts(h):
        return [(n, h * PAIR, 2 * stride) for n in range(2)]

    kv = list(interleave(apart, (key_rows, value_rows), members, HEAD_DIM, [(True, kv_parts)]))
    sets = [(h == 0, qo_parts(h)) for h in range(heads)]
    packed = interleave(apart, (queries, grad_out), members, PAIR, sets)
    late = order[EARLY]
    kv[late], (*first, second) = lax.optimization_barrier((kv[late], packed))
    kv = swap(kv, None, 5)
    first = swap(first, kv, 5)
    own = assemble(apart, kv, heads)
    second, first[order[HOLD]] = lax.optimization_barrier((second, first[order[HOLD]]))
    qos = [first, [exchange(second).reshape(WINDOW, -1)]]
    held, first[order[-2]] = lax.optimization_barrier((own[1], first[order[-2]]))
    halos = [onward(own[0]), onward(held)]
    outs, mine, back = [], [], []
    for h in range(heads):
        last = h == heads - 1
        *ao, dhalo, down = attention(apart, qos[h], halos[h], own[h], members if last else 1)
        if last:
            ao[order[WAITS]], back[h - 1] = lax.optimization_barrier((ao[order[WAITS]], back[h - 1]))
        back.append(backward(dhalo, not last))
        outs.append(swap(ao) if last else exchange(ao[0].reshape(members, rows, -1)))
        mine.append(down)
    total = add(apart, *settle(mine, back[0]), back[1], members)
    outs[0], total = lax.optimization_barrier((outs[0], total))
    grad_k, grad_v = unpack(apart, swap(total, outs[-1], 5))
    attended, grad_q = spread(apart, *outs)
    return (attended, grad_q, grad_k, grad_v)


def solution(mesh):
    placed = P(("seq", "kvh"), None)
    return jax.shard_map(
        body, mesh=mesh, in_specs=(placed,) * 4, out_specs=(placed,) * 4, check_vma=False
    )
```
